512 devices in a mesh: section: 16 (over y, x_lo), dp: 32 (over x_hi, z, core).
Axes of the slice: x: 4 (x_hi: 2, x_lo: 2; x = x_hi * 2 + x_lo), y: 8, z: 8, core: 2. Of those that a mesh axis runs over, the one named last changes fastest.
Arguments:
- inputs: bfloat16 [64, 512, 1024], P('dp', None, 'section'), may hold values from -6 to 6
- cotangent: bfloat16 [64, 512, 1024], P('dp', None, 'section'), may hold values from -6 to 6
- weights: bfloat16 [16, 1024, 1024], P('section'), may hold values from -0.09375 to 0.09375
- proj_in: bfloat16 [16, 1024, 64], P('section'), may hold values from -0.1875 to 0.1875
- proj_out: bfloat16 [16, 1024, 64], P('section'), may hold values from -0.1875 to 0.1875
- query_factors: bfloat16 [16, 512, 4096], P('section', 'dp'), may hold values from -0.0009765625 to 0.0009765625
Outputs:
- scores: float32 [64, 512], P('section', 'dp')
The draws below stay inside these ranges and needn't reach their ends.
All inputs are finite; a program needn't handle non-finite values.
Results may differ from the reference program's by a relative error of at most 0.02.
Values may be sent and summed in bfloat16 or wider, within the bound.
No kernel may reach another device: no remote copies, remote signals or barrier semaphores. Data moves between devices by JAX's collectives and lax.ppermute only.
A program may use at most 64 MiB of HBM per device.

```python
import jax
import jax.numpy as jnp
from jax import lax

D = 1024
RANK = 64
SEQ = 512
LAYERS = 16
EXAMPLES = 64
QUERIES = 512


def shard_levels(rng, dims, split, smallest, top_value):
    factor_of, own = 1.0, jax.random.fold_in(rng, 6)
    for position, blocks in split:
        steps = jnp.exp(jax.random.uniform(jax.random.fold_in(own, position), (blocks,), jnp.float32, smallest / len(split), top_value / len(split)))
        factor_of = factor_of * jnp.repeat(steps, dims[position] // blocks).reshape([-1 if axis == position else 1 for axis in range(len(dims))])
    return factor_of


def scatter_about(key, extent, scale, reach, split=(), kind=jnp.bfloat16):
    level = shard_levels(key, extent, split, -0.22, 0.18) if split else 1.0
    result = jax.random.normal(key, extent, jnp.float32) * scale * level
    return jnp.minimum(jnp.maximum(result, -reach), reach).astype(kind)


def setup_inputs(seed: int = 0) -> dict:
    keys = jax.random.split(jax.random.key(seed), 7)
    return {
        "inputs": scatter_about(keys[0], (EXAMPLES, SEQ, D), 1.0, 6.0, ((0, 32), (2, 16))),
        "cotangent": scatter_about(keys[1], (EXAMPLES, SEQ, D), 1.0, 6.0, ((0, 32), (2, 16))),
        "weights": scatter_about(keys[2], (LAYERS, D, D), (4 * D) ** -0.5, 0.09375, ((0, 16),)),
        "proj_in": scatter_about(keys[3], (LAYERS, D, RANK), D ** -0.5, 0.1875, ((0, 16),)),
        "proj_out": scatter_about(keys[4], (LAYERS, D, RANK), D ** -0.5, 0.1875, ((0, 16),)),
        "query_factors": scatter_about(keys[5], (LAYERS, QUERIES, RANK * RANK), (SEQ * RANK * RANK * LAYERS) ** -0.5, 0.0009765625, ((0, 16), (1, 32))),
    }


def forward_layer(hidden, weight):
    preact = jnp.dot(hidden, weight, preferred_element_type=jnp.float32)
    return (hidden.astype(jnp.float32) + jax.nn.silu(preact)).astype(jnp.bfloat16)


def backward_layer(hidden, upstream, weight, left_map, right_map):
    preact = jnp.dot(hidden, weight, preferred_element_type=jnp.float32)
    sigmoid_vals = jax.nn.sigmoid(preact)
    pre_grad = (upstream.astype(jnp.float32) * sigmoid_vals * (1.0 + preact * (1.0 - sigmoid_vals))).astype(jnp.bfloat16)
    carried = lax.dot_general(pre_grad, weight, (((1,), (1,)), ((), ())), preferred_element_type=jnp.float32)
    downstream = (upstream.astype(jnp.float32) + carried).astype(jnp.bfloat16)
    left_proj = jnp.dot(hidden, left_map, preferred_element_type=jnp.float32)
    right_proj = jnp.dot(pre_grad, right_map, preferred_element_type=jnp.float32)
    factor = lax.dot_general(left_proj, right_proj, (((0,), (0,)), ((), ())), precision=lax.Precision.HIGHEST, preferred_element_type=jnp.float32)
    return downstream, factor.reshape(-1)


def reference(inputs, cotangent, weights, proj_in, proj_out, query_factors):
    def one_sequence(pair):
        hidden, upstream = pair
        saved = []
        for layer in range(LAYERS):
            saved.append(hidden)
            hidden = forward_layer(hidden, weights[layer])
        collected = [None] * LAYERS
        for layer in reversed(range(LAYERS)):
            upstream, factor = backward_layer(saved[layer], upstream, weights[layer], proj_in[layer], proj_out[layer])
            collected[layer] = factor
        return jnp.stack(collected, axis=0)

    factors = lax.map(one_sequence, (inputs, cotangent))
    scores = jnp.zeros((inputs.shape[0], query_factors.shape[1]), jnp.float32)
    for layer in range(LAYERS):
        table = lax.dot_general(factors[:, layer, :], query_factors[layer].astype(jnp.float32), (((1,), (1,)), ((), ())), precision=lax.Precision.HIGHEST, preferred_element_type=jnp.float32)
        scores = scores + table
    return scores
```

```python
import functools

import jax
import jax.numpy as jnp
from jax import lax
from jax.experimental import pallas as pl
from jax.experimental.pallas import tpu as pltpu
from jax.sharding import PartitionSpec as P

AXES = ("section", "dp")
TOK = 128
STAGE = 8
D = 1024
RANK = 64
PACK = D + 2 * RANK
PIECE = 128


def flat(x, y, z, c):
    return (y % 8 * 2 + x % 2) * 32 + ((x % 4 // 2) * 8 + z % 8) * 2 + c


def pairs(target):
    out = []
    for x in range(4):
        for y in range(8):
            for z in range(8):
                for c in range(2):
                    to = target(x, y, z, c)
                    if to is not None:
                        out.append((flat(x, y, z, c), flat(*to)))
    return out


def move(value, target):
    return lax.ppermute(value, AXES, pairs(target))


def swap_core(value):
    return move(value, lambda x, y, z, c: (x, y, z, 1 - c))


BUFFERS = []
for core_flag in (0, 1):
    for column_flag, quarter in ((0, 0), (0, 1), (0, 3), (1, 0), (1, 2), (1, 1), (1, 3), (0, 2)):
        BUFFERS.append((column_flag, core_flag, quarter))


def gather_stage(pack, core, quarter):
    half = lax.dynamic_slice_in_dim(pack, core * (D // 2), D // 2, 0)
    piece = lax.dynamic_slice_in_dim(pack, (core * 4 + quarter) * PIECE, PIECE, 0)
    rows = [
        move(piece, lambda x, y, z, c, r=r: (x, y // 4 * 4 + (y + r) % 4, z, c)) for r in (1, 2, 3)
    ]
    beside = move(half, lambda x, y, z, c: (x + 1 if c == 0 else x - 1, y, z, c))
    beside_other = swap_core(beside)
    own = jnp.stack(rows)
    above = move(own, lambda x, y, z, c: (x, y, z - 1, c))
    below = move(own, lambda x, y, z, c: (x, y, z + 1, c))
    near = move(own, lambda x, y, z, c: (x ^ 1, y, z, c))
    far = move(own, lambda x, y, z, c: (3 - x, y, z, c))
    near_above = move(near, lambda x, y, z, c: (x, y, z - 1, c))
    near_below = move(near, lambda x, y, z, c: (x, y, z + 1, c))
    own_far = move(far, lambda x, y, z, c: (x ^ 1, y, z, c))
    mine = [own, above, below, near, far, near_above, near_below, own_far]
    return [beside, beside_other] + mine + [swap_core(value) for value in mine]


def load_layers(place, pack, beside, buffers, layers, sems, reverse):
    row, col, core, quarter = (place[k] for k in range(4))
    for step in range(4):
        source_row = 3 - step if reverse else step
        distance = (row - source_row) & 3
        mine, other = source_row * 2 + col, source_row * 2 + 1 - col

        @pl.when(distance == 0)
        def _():
            pltpu.make_async_copy(pack, layers.at[mine], sems.at[mine]).start()
            for flag in (0, 1):
                side = jnp.where(flag == 0, core, 1 - core)
                rows = pl.ds(pl.multiple_of(side * (D // 2), D // 2), D // 2)
                pltpu.make_async_copy(
                    beside[flag], layers.at[other, rows], sems.at[other]
                ).start()

        @pl.when(distance > 0)
        def _():
            for (column_flag, core_flag, shift), ref in zip(BUFFERS, buffers):
                slot = other if column_flag else mine
                side = 1 - core if core_flag else core
                piece = side * 4 + ((quarter + shift) & 3)
                rows = pl.ds(pl.multiple_of(piece * PIECE, PIECE), PIECE)
                pltpu.make_async_copy(
                    ref.at[distance - 1], layers.at[slot, rows], sems.at[slot]
                ).start()


def await_layer(layers, sems, slot):
    pltpu.make_async_copy(layers.at[slot], layers.at[slot], sems.at[slot]).wait()


def forward_one(slot, hidden, layers, slope, left):
    both = jnp.dot(hidden, layers[slot], preferred_element_type=jnp.float32)
    preact = both[:, :D]
    sig = jax.nn.sigmoid(preact)
    slope[slot] = sig * (1.0 + preact * (1.0 - sig))
    left[slot] = both[:, D:]
    return (hidden.astype(jnp.float32) + preact * sig).astype(jnp.bfloat16)


def backward_one(slot, upstream, layers, slope, left, factor):
    wide = upstream.astype(jnp.float32)
    grad = (wide * slope[slot]).astype(jnp.bfloat16)
    right = jnp.dot(grad, layers[slot, :, D:], preferred_element_type=jnp.float32)
    carried = lax.dot_general(
        grad, layers[slot, :, :D], (((1,), (1,)), ((), ())), preferred_element_type=jnp.float32
    )
    product = lax.dot_general(
        left[slot],
        right,
        (((0,), (0,)), ((), ())),
        precision=lax.Precision.HIGHEST,
        preferred_element_type=jnp.float32,
    )
    factor[slot] = product[:RANK, RANK:].astype(jnp.bfloat16)
    return (wide + carried).astype(jnp.bfloat16)


def rows_of(arrived):
    return jnp.concatenate([arrived[k] for k in range(arrived.shape[0])], axis=1)


def first_kernel(place, arrived, pack, *refs):
    beside, buffers = refs[:2], refs[2:18]
    hidden_out, slope, left, layers, sems = refs[18:]

    @pl.when(place[4] == 0)
    def _():
        load_layers(place, pack, beside, buffers, layers, sems, False)
        hidden_out[...] = rows_of(arrived)

        def body(slot, carry):
            await_layer(layers, sems, slot)
            hidden_out[...] = forward_one(slot, hidden_out[...], layers, slope, left)
            return carry

        lax.fori_loop(0, STAGE, body, 0)


def middle_kernel(place, hidden, arrived, pack, *refs):
    beside, buffers = refs[:2], refs[2:18]
    upstream, factor, current, slope, left, layers, sems = refs[18:]

    @pl.when(place[4] == 1)
    def _():
        load_layers(place, pack, beside, buffers, layers, sems, False)
        current[...] = hidden[...]
        upstream[...] = rows_of(arrived)

        def ahead(slot, carry):
            await_layer(layers, sems, slot)
            current[...] = forward_one(slot, current[...], layers, slope, left)
            return carry

        lax.fori_loop(0, STAGE, ahead, 0)

        def back(step, carry):
            slot = STAGE - 1 - step
            upstream[...] = backward_one(slot, upstream[...], layers, slope, left, factor)
            return carry

        lax.fori_loop(0, STAGE, back, 0)


def last_kernel(place, upstream, slope, left, pack, *refs):
    beside, buffers = refs[:2], refs[2:18]
    factor, current, layers, sems = refs[18:]

    @pl.when(place[4] == 0)
    def _():
        load_layers(place, pack, beside, buffers, layers, sems, True)
        current[...] = upstream[...]

        def back(step, carry):
            slot = STAGE - 1 - step
            await_layer(layers, sems, slot)
            current[...] = backward_one(slot, current[...], layers, slope, left, factor)
            return carry

        lax.fori_loop(0, STAGE, back, 0)


VMEM = pl.BlockSpec(memory_space=pltpu.VMEM)
SMEM = pl.BlockSpec(memory_space=pltpu.SMEM)
HBM = pl.BlockSpec(memory_space=pl.ANY)
PARAMS = pltpu.CompilerParams(vmem_limit_bytes=48 * 1024 * 1024)
TOKENS = jax.ShapeDtypeStruct((TOK, D), jnp.bfloat16)
SLOPE = jax.ShapeDtypeStruct((STAGE, TOK, D), jnp.float32)
LEFT = jax.ShapeDtypeStruct((STAGE, TOK, 2 * RANK), jnp.float32)
FACTOR = jax.ShapeDtypeStruct((STAGE, RANK, RANK), jnp.bfloat16)
LAYERS = pltpu.VMEM((STAGE, D, PACK), jnp.bfloat16)
SEMS = pltpu.SemaphoreType.DMA((STAGE,))


def scratch(shape):
    return pltpu.VMEM(shape.shape, shape.dtype)


def cost(passes):
    return pl.CostEstimate(
        flops=2 * passes * STAGE * TOK * D * PACK,
        bytes_accessed=STAGE * D * PACK * 2,
        transcendentals=STAGE * TOK * D,
    )


def on_device(inputs, cotangent, weights, proj_in, proj_out, query_factors):
    section, dp = lax.axis_index("section"), lax.axis_index("dp")
    y, col = section // 2, section % 2
    x_hi, z, core = dp // 16, dp // 2 % 8, dp % 2
    stage = y // 4
    quarter = (z + 2 * x_hi) % 4
    place = jnp.stack([y % 4, col, core, quarter, stage]).astype(jnp.int32)

    ahead = inputs.reshape(STAGE, TOK, -1)
    seeds = cotangent.reshape(4, 2, TOK, -1)[::-1].reshape(STAGE, TOK, -1)
    arrived = lax.all_to_all(
        jnp.concatenate([ahead, seeds]), "section", 0, 0, tiled=True
    )

    pack = jnp.concatenate([weights[0], proj_in[0], proj_out[0]], axis=1)
    gathered = gather_stage(pack, core, quarter)

    across = [[(h * 8 + k) * 2 + c for h in range(2) for c in range(2)] for k in range(8)]
    along = [[(h * 8 + k) * 2 + c for k in range(8)] for h in range(2) for c in range(2)]
    local = query_factors[0]
    queries = lax.all_to_all(
        jnp.broadcast_to(local[None], (4,) + local.shape),
        "dp",
        0,
        0,
        tiled=True,
        axis_index_groups=across,
    ).reshape(4 * local.shape[0], -1)

    hidden, slope, left = pl.pallas_call(
        first_kernel,
        out_shape=(TOKENS, SLOPE, LEFT),
        in_specs=[SMEM, VMEM] + [HBM] * 19,
        out_specs=(VMEM, VMEM, VMEM),
        scratch_shapes=[LAYERS, SEMS],
        compiler_params=PARAMS,
        cost_estimate=cost(1),
        name="forward_first_stage",
    )(place, arrived, pack, *gathered)
    hidden = move(hidden, lambda x, y, z, c: (x, 7 - y, z, c) if y < 4 else None)
    upstream, factor_late = pl.pallas_call(
        middle_kernel,
        out_shape=(TOKENS, FACTOR),
        in_specs=[SMEM, VMEM, VMEM] + [HBM] * 19,
        out_specs=(VMEM, VMEM),
        scratch_shapes=[scratch(TOKENS), scratch(SLOPE), scratch(LEFT), LAYERS, SEMS],
        compiler_params=PARAMS,
        cost_estimate=cost(2),
        name="second_stage",
    )(place, hidden, arrived, pack, *gathered)
    upstream = move(upstream, lambda x, y, z, c: (x, 7 - y, z, c) if y > 3 else None)
    factor_early = pl.pallas_call(
        last_kernel,
        out_shape=FACTOR,
        in_specs=[SMEM, VMEM, VMEM, VMEM] + [HBM] * 19,
        out_specs=VMEM,
        scratch_shapes=[scratch(TOKENS), LAYERS, SEMS],
        compiler_params=PARAMS,
        cost_estimate=cost(1),
        name="backward_first_stage",
    )(place, upstream, slope, left, pack, *gathered)

    factor = jnp.where(stage == 0, factor_early, factor_late).reshape(STAGE, -1)
    groups = [list(range(8)), list(range(8, 16))]
    parts = lax.all_to_all(factor, "section", 0, 0, tiled=True, axis_index_groups=groups)
    sums = parts.reshape(2, 4, -1).astype(jnp.float32).sum(1)
    sums = jnp.where(stage == 0, sums, sums[::-1]).astype(jnp.bfloat16)
    sums = lax.all_to_all(
        jnp.broadcast_to(sums[None], (8,) + sums.shape),
        "dp",
        0,
        0,
        tiled=True,
        axis_index_groups=along,
    ).reshape(16, -1)
    table = lax.dot_general(
        sums, queries, (((1,), (1,)), ((), ())), preferred_element_type=jnp.float32
    ).reshape(8, 2, -1)

    outgoing = lax.dynamic_update_slice_in_dim(
        jnp.zeros((16,) + table.shape[1:], jnp.float32), table, x_hi * 8, 0
    )
    scores = lax.all_to_all(outgoing, "section", 0, 0, tiled=True).sum(0)
    scores = scores.reshape(2, 4, -1).transpose(1, 0, 2)
    scores = lax.all_to_all(scores, "dp", 0, 0, tiled=True, axis_index_groups=across)
    return scores.reshape(2, 4, -1).sum(0)


def solution(mesh):
    placed = (
        P("dp", None, "section"),
        P("dp", None, "section"),
        P("section", None, None),
        P("section", None, None),
        P("section", None, None),
        P("section", "dp", None),
    )
    return jax.shard_map(
        on_device, mesh=mesh, in_specs=placed, out_specs=P("section", "dp"), check_vma=False
    )
```

```python
import functools

import jax
import jax.numpy as jnp
from jax import lax
from jax.experimental import pallas as pl
from jax.experimental.pallas import tpu as pltpu
from jax.sharding import PartitionSpec as P

AXES = ("section", "dp")
TOK = 128
STAGE = 8
D = 1024
RANK = 64
PACK = D + 2 * RANK
PIECE = PACK // 8


def flat(x, y, z, c):
    return (y % 8 * 2 + x % 2) * 32 + ((x % 4 // 2) * 8 + z % 8) * 2 + c


def pairs(target):
    out = []
    for x in range(4):
        for y in range(8):
            for z in range(8):
                for c in range(2):
                    to = target(x, y, z, c)
                    if to is not None:
                        out.append((flat(x, y, z, c), flat(*to)))
    return out


def move(value, target):
    return lax.ppermute(value, AXES, pairs(target))


def swap_core(value):
    return move(value, lambda x, y, z, c: (x, y, z, 1 - c))


def gather_rows(pack, core, quarter):
    piece = lax.dynamic_slice_in_dim(pack, (core * 4 + quarter) * PIECE, PIECE, 0)
    rows = [
        move(piece, lambda x, y, z, c, r=r: (x, y // 4 * 4 + (y + r) % 4, z, c)) for r in (1, 2, 3)
    ]
    half = lax.dynamic_slice_in_dim(pack, core * (PACK // 2), PACK // 2, 0)
    beside = move(half, lambda x, y, z, c: (x + 1 if c == 0 else x - 1, y, z, c))
    return rows, beside


def along_z(value):
    return move(value, lambda x, y, z, c: (x, y, z + 1 - 2 * (c ^ (x // 2)), c))


def along_x(value):
    return move(value, lambda x, y, z, c: (x ^ 1 if c == 0 else 3 - x, y, z, c))


def assemble(place, pieces, halves, whole, layers, sems):
    row, col, core = (place[k] for k in range(3))
    copies = []

    def put(source, slot, rows):
        target = layers.at[slot] if rows is None else layers.at[slot, rows]
        copies.append(pltpu.make_async_copy(source, target, sems.at[len(copies)]))

    if whole is not None:
        put(whole, row * 2 + col, None)
    for half, ref in halves:
        put(ref, row * 2 + 1 - col, pl.ds(pl.multiple_of(half * (PACK // 2), PACK // 2), PACK // 2))
    for distance in (1, 2, 3):
        source_row = (row - distance) & 3
        for source, other_col, other_core, quarter in pieces:
            slot = source_row * 2 + (1 - col if other_col else col)
            half = 1 - core if other_core else core
            start = pl.multiple_of((half * 4 + (quarter & 3)) * PIECE, PIECE)
            put(source.at[distance - 1], slot, pl.ds(start, PIECE))
    for copy in copies:
        copy.start()
    for copy in copies:
        copy.wait()


def early_kernel(place, pack, beside, own, own_other, up, up_more, side, side_more, layers, sems):
    core, quarter, way = (place[k] for k in (2, 3, 4))
    pieces = [
        (own, 0, 0, quarter),
        (own_other, 0, 1, quarter),
        (up, 0, 0, quarter - way),
        (up_more, 0, 1, quarter - way),
        (side, 1, 0, quarter + 2 * core),
        (side_more, 1, 1, quarter + 2 * core),
    ]
    assemble(place, pieces, ((core, beside),), pack, layers, sems)


def late_kernel(
    place, beside, up, up_more, side, side_more, turn, turn_more, turn_other, turn_more_other,
    two, two_more, before, layers, sems
):
    core, quarter, way = (place[k] for k in (2, 3, 4))
    pieces = [
        (up, 0, 1, quarter + way),
        (up_more, 0, 0, quarter + way),
        (side, 1, 1, quarter + 2 * (1 - core)),
        (side_more, 1, 0, quarter + 2 * (1 - core)),
        (turn, 1, 0, quarter - way),
        (turn_more, 1, 1, quarter - way),
        (turn_other, 1, 1, quarter + way),
        (turn_more_other, 1, 0, quarter + way),
        (two, 0, 0, quarter + 2),
        (two_more, 0, 1, quarter + 2),
    ]
    assemble(place, pieces, ((1 - core, beside),), None, layers, sems)


CHUNK = 256


def forward_one(slot, current, layers, slope, left):
    hidden = current[...]
    left[slot] = lax.dot_general(
        layers[slot, D:], hidden, (((1,), (1,)), ((), ())), preferred_element_type=jnp.float32
    )
    for start in range(0, D, CHUNK):
        cols = slice(start, start + CHUNK)
        preact = jnp.dot(hidden, layers[slot, :D, cols], preferred_element_type=jnp.float32)
        sig = jax.nn.sigmoid(preact)
        slope[slot, :, cols] = sig * (1.0 + preact * (1.0 - sig))
        current[:, cols] = (hidden[:, cols].astype(jnp.float32) + preact * sig).astype(jnp.bfloat16)


def backward_one(slot, current, layers, slope, left, factor):
    upstream = current[...].astype(jnp.float32)
    grad = (upstream * slope[slot]).astype(jnp.bfloat16)
    nt = (((1,), (1,)), ((), ()))
    right = lax.dot_general(grad, layers[slot, D:], nt, preferred_element_type=jnp.float32)
    product = jnp.dot(
        left[slot],
        right,
        precision=lax.Precision.HIGHEST,
        preferred_element_type=jnp.float32,
    )
    factor[slot] = product[:RANK, RANK:].astype(jnp.bfloat16)
    for start in range(0, D, CHUNK):
        cols = slice(start, start + CHUNK)
        carried = lax.dot_general(
            grad, layers[slot, cols], nt, preferred_element_type=jnp.float32
        )
        current[:, cols] = (upstream[:, cols] + carried).astype(jnp.bfloat16)


def rows_of(arrived):
    return arrived[...].reshape(D, TOK).T


def first_kernel(place, arrived, layers, current, slope_out, left, slope, sems):
    def keep(slot):
        return pltpu.make_async_copy(slope.at[slot], slope_out.at[slot], sems.at[slot])

    @pl.when(place[5] == 0)
    def _():
        current[...] = rows_of(arrived)

        def body(slot, carry):
            forward_one(slot, current, layers, slope, left)
            keep(slot).start()
            return carry

        lax.fori_loop(0, STAGE, body, 0)
        for slot in range(STAGE):
            keep(slot).wait()


def middle_kernel(place, hidden, arrived, layers, upstream, factor, current, slope, left):
    @pl.when(place[5] == 1)
    def _():
        current[...] = hidden[...]
        upstream[...] = rows_of(arrived)

        def ahead(slot, carry):
            forward_one(slot, current, layers, slope, left)
            return carry

        lax.fori_loop(0, STAGE, ahead, 0)

        def back(step, carry):
            backward_one(STAGE - 1 - step, upstream, layers, slope, left, factor)
            return carry

        lax.fori_loop(0, STAGE, back, 0)


def last_kernel(place, upstream, slope_in, left, late, layers_in, factor, current, slope, layers, sems):
    def fetch(slot):
        return (
            pltpu.make_async_copy(slope_in.at[slot], slope.at[slot], sems.at[0, slot]),
            pltpu.make_async_copy(layers_in.at[slot], layers.at[slot], sems.at[1, slot]),
        )

    @pl.when(place[5] == 0)
    def _():
        for slot in reversed(range(STAGE)):
            for copy in fetch(slot):
                copy.start()
        current[...] = upstream[...]

        def back(step, carry):
            slot = STAGE - 1 - step
            for copy in fetch(slot):
                copy.wait()
            backward_one(slot, current, layers, slope, left, factor)
            return carry

        lax.fori_loop(0, STAGE, back, 0)

    @pl.when(place[5] == 1)
    def _():
        factor[...] = late[...]


VMEM = pl.BlockSpec(memory_space=pltpu.VMEM)
SMEM = pl.BlockSpec(memory_space=pltpu.SMEM)
ANY = pl.BlockSpec(memory_space=pl.ANY)
HBM = pl.BlockSpec(memory_space=pltpu.HBM)
PARAMS = pltpu.CompilerParams(vmem_limit_bytes=10 * 1024 * 1024)
LARGE = pltpu.CompilerParams(vmem_limit_bytes=30 * 1024 * 1024)
TOKENS = jax.ShapeDtypeStruct((TOK, D), jnp.bfloat16)
SLOPE = jax.ShapeDtypeStruct((STAGE, TOK, D), jnp.float32)
LEFT = jax.ShapeDtypeStruct((STAGE, 2 * RANK, TOK), jnp.float32)
FACTOR = jax.ShapeDtypeStruct((STAGE, RANK, RANK), jnp.bfloat16)
LAYERS = jax.ShapeDtypeStruct((STAGE, PACK, D), jnp.bfloat16)


def scratch(shape):
    return pltpu.VMEM(shape.shape, shape.dtype)


def cost(passes):
    return pl.CostEstimate(
        flops=2 * passes * STAGE * TOK * D * PACK,
        bytes_accessed=STAGE * D * PACK * 2,
        transcendentals=STAGE * TOK * D,
    )


def on_device(inputs, cotangent, weights, proj_in, proj_out, query_factors):
    section, dp = lax.axis_index("section"), lax.axis_index("dp")
    y, col = section // 2, section % 2
    x_hi, z, core = dp // 16, dp // 2 % 8, dp % 2
    stage = y // 4
    quarter = (z + 2 * x_hi) % 4
    way = 1 - 2 * (core ^ x_hi)
    place = jnp.stack([y % 4, col, core, quarter, way, stage]).astype(jnp.int32)

    pack = jnp.concatenate([weights[0], proj_in[0].T, proj_out[0].T])
    rows, beside = gather_rows(pack, core, quarter)

    ahead, seeds = (
        value.reshape(2, 4, TOK, -1).transpose(0, 1, 3, 2).reshape(STAGE, -1, TOK)
        for value in (inputs, cotangent)
    )
    order = [ahead] + [seeds[k : k + 2] for k in (6, 4, 2, 0)]
    rows[0], order = lax.optimization_barrier((rows[0], jnp.concatenate(order)))
    arrived = lax.all_to_all(order, "section", 0, 0, tiled=True)

    own = jnp.stack(rows)
    up, side = along_z(own), along_x(own)
    own_other = swap_core(own)
    own_other, beside = lax.optimization_barrier((own_other, beside))
    up_more, side_more = along_z(own_other), along_x(own_other)
    turn, two = along_x(up), along_z(up)
    turn, two, up_more, side_more, arrived = lax.optimization_barrier(
        (turn, two, up_more, side_more, arrived)
    )
    turn_more, two_more = along_x(up_more), along_z(up_more)
    layers = pl.pallas_call(
        early_kernel,
        out_shape=LAYERS,
        in_specs=[SMEM] + [ANY] * 8,
        out_specs=VMEM,
        scratch_shapes=[pltpu.SemaphoreType.DMA((20,))],
        compiler_params=PARAMS,
        name="place_early_pieces",
    )(place, pack, beside, own, own_other, up, up_more, side, side_more)
    swapped = [swap_core(value) for value in (beside, up, up_more, side, side_more)]
    queries = query_factors
    layers, queries = lax.optimization_barrier((layers, queries))
    queries = jnp.concatenate([queries, swap_core(queries)])
    queries = jnp.concatenate([queries, move(queries, lambda x, y, z, c: (x ^ 2, y, z, c))])
    layers = pl.pallas_call(
        late_kernel,
        out_shape=LAYERS,
        in_specs=[SMEM] + [ANY] * 11 + [VMEM],
        out_specs=VMEM,
        scratch_shapes=[pltpu.SemaphoreType.DMA((31,))],
        input_output_aliases={12: 0},
        compiler_params=PARAMS,
        name="place_late_pieces",
    )(
        place, *swapped, turn, turn_more, swap_core(turn), swap_core(turn_more), two, two_more, layers
    )

    hidden, slope, left = pl.pallas_call(
        first_kernel,
        out_shape=(TOKENS, SLOPE, LEFT),
        in_specs=[SMEM, VMEM, VMEM],
        out_specs=(VMEM, HBM, VMEM),
        scratch_shapes=[scratch(SLOPE), pltpu.SemaphoreType.DMA((STAGE,))],
        compiler_params=PARAMS,
        cost_estimate=cost(1),
        name="forward_first_stage",
    )(place, arrived, layers)
    hidden = move(hidden, lambda x, y, z, c: (x, 7 - y, z, c) if y < 4 else None)
    upstream, factor_late = pl.pallas_call(
        middle_kernel,
        out_shape=(TOKENS, FACTOR),
        in_specs=[SMEM, VMEM, VMEM, VMEM],
        out_specs=(VMEM, VMEM),
        scratch_shapes=[scratch(TOKENS), scratch(SLOPE), scratch(LEFT)],
        compiler_params=PARAMS,
        cost_estimate=cost(2),
        name="second_stage",
    )(place, hidden, arrived, layers)
    upstream = move(upstream, lambda x, y, z, c: (x, 7 - y, z, c) if y > 3 else None)
    upstream, queries = lax.optimization_barrier((upstream, queries))
    factor = pl.pallas_call(
        last_kernel,
        out_shape=FACTOR,
        in_specs=[SMEM, VMEM, HBM, VMEM, VMEM, HBM],
        out_specs=VMEM,
        scratch_shapes=[
            scratch(TOKENS),
            scratch(SLOPE),
            scratch(LAYERS),
            pltpu.SemaphoreType.DMA((2, STAGE)),
        ],
        compiler_params=LARGE,
        cost_estimate=cost(1),
        name="backward_first_stage",
    )(place, upstream, slope, left, factor_late, pltpu.with_memory_space_constraint(layers, pltpu.HBM))

    factor = factor.reshape(STAGE, -1)
    groups = [list(range(8)), list(range(8, 16))]
    parts = lax.all_to_all(factor, "section", 0, 0, tiled=True, axis_index_groups=groups)
    low, high = parts.reshape(2, 4, -1).astype(jnp.float32).sum(1)
    along = [[(h * 8 + k) * 2 + c for k in range(8)] for h in range(2) for c in range(2)]
    sums = jnp.stack([jnp.where(stage == 0, low, high), jnp.where(stage == 0, high, low)])
    sums = sums.astype(jnp.bfloat16)
    sums = lax.all_to_all(
        jnp.broadcast_to(sums[None], (8,) + sums.shape),
        "dp",
        0,
        0,
        tiled=True,
        axis_index_groups=along,
    ).reshape(16, -1)
    table = lax.dot_general(
        sums, queries.reshape(-1, sums.shape[1]), (((1,), (1,)), ((), ())),
        preferred_element_type=jnp.float32,
    ).reshape(16, 2, 2, -1)
    table = jnp.where(x_hi == 0, table, table[:, ::-1])
    table = jnp.where(core == 0, table, table[:, :, ::-1]).reshape(8, 2, -1)

    outgoing = lax.dynamic_update_slice_in_dim(
        jnp.zeros((16,) + table.shape[1:], jnp.float32), table, x_hi * 8, 0
    )
    across = [[(h * 8 + k) * 2 + c for h in range(2) for c in range(2)] for k in range(8)]
    scores = lax.all_to_all(outgoing, "section", 0, 0, tiled=True).sum(0)
    scores = scores.reshape(2, 4, -1).transpose(1, 0, 2)
    scores = lax.all_to_all(scores, "dp", 0, 0, tiled=True, axis_index_groups=across)
    return scores.reshape(2, 4, -1).sum(0)


def solution(mesh):
    placed = (
        P("dp", None, "section"),
        P("dp", None, "section"),
        P("section", None, None),
        P("section", None, None),
        P("section", None, None),
        P("section", "dp", None),
    )
    return jax.shard_map(
        on_device, mesh=mesh, in_specs=placed, out_specs=P("section", "dp"), check_vma=False
    )
```

```python
import functools

import jax
import jax.numpy as jnp
from jax import lax
from jax.experimental import pallas as pl
from jax.experimental.pallas import tpu as pltpu
from jax.sharding import PartitionSpec as P

AXES = ("section", "dp")
TOK = 128
STAGE = 8
D = 1024
RANK = 64
PACK = D + 2 * RANK
PIECE = PACK // 8


def flat(x, y, z, c):
    return (y % 8 * 2 + x % 2) * 32 + ((x % 4 // 2) * 8 + z % 8) * 2 + c


def pairs(target):
    out = []
    for x in range(4):
        for y in range(8):
            for z in range(8):
                for c in range(2):
                    to = target(x, y, z, c)
                    if to is not None:
                        out.append((flat(x, y, z, c), flat(*to)))
    return out


def move(value, target):
    return lax.ppermute(value, AXES, pairs(target))


def swap_core(value):
    return move(value, lambda x, y, z, c: (x, y, z, 1 - c))


def gather_rows(pack, core, quarter):
    piece = lax.dynamic_slice_in_dim(pack, (core * 4 + quarter) * PIECE, PIECE, 0)
    rows = [
        move(piece, lambda x, y, z, c, r=r: (x, y // 4 * 4 + (y + r) % 4, z, c)) for r in (1, 2, 3)
    ]
    half = lax.dynamic_slice_in_dim(pack, core * (PACK // 2), PACK // 2, 0)
    beside = move(half, lambda x, y, z, c: (x + 1 if c == 0 else x - 1, y, z, c))
    return rows, beside


def along_z(value):
    return move(value, lambda x, y, z, c: (x, y, z + 1 - 2 * (c ^ (x // 2)), c))


def along_x(value):
    return move(value, lambda x, y, z, c: (x ^ 1 if c == 0 else 3 - x, y, z, c))


def assemble(place, pieces, beside, whole, extra, layers, sems):
    row, col, core = (place[k] for k in range(3))
    copies = []

    def put(source, target):
        copies.append(pltpu.make_async_copy(source, target, sems.at[len(copies)]))

    def rows(piece):
        return pl.ds(pl.multiple_of(piece * PIECE, PIECE), PIECE)

    if whole is not None:
        put(whole, layers.at[row * 2 + col])
    half, refs = beside
    for k in range(4):
        put(refs[k // 2].at[k % 2], layers.at[row * 2 + 1 - col, rows(half * 4 + k)])
    for distance in (1, 2, 3):
        source_row = (row - distance) & 3
        for ref, index, other_col, other_core, quarter in pieces:
            slot = source_row * 2 + (1 - col if other_col else col)
            half = 1 - core if other_core else core
            put(ref.at[index + distance - 1], layers.at[slot, rows(half * 4 + (quarter & 3))])
    for source, target in extra:
        put(source, target)
    for copy in copies:
        copy.start()
    for copy in copies:
        copy.wait()


def early_kernel(place, pack, beside, own, up, side, layers, first, second, sems):
    core, quarter, way = (place[k] for k in (2, 3, 4))
    pieces = []
    for k in (0, 1):
        pieces.append((own.at[k], 0, 0, k, quarter))
        pieces.append((up, 3 * k, 0, k, quarter - way))
        pieces.append((side, 3 * k, 1, k, quarter + 2 * core))
    extra = [
        (beside.at[pl.ds(0, 2)], first.at[pl.ds(0, 2)]),
        (beside.at[pl.ds(2, 2)], second.at[pl.ds(0, 2)]),
        (up, first.at[pl.ds(2, 6)]),
        (side, second.at[pl.ds(2, 6)]),
    ]
    assemble(place, pieces, (core, (beside.at[pl.ds(0, 2)], beside.at[pl.ds(2, 2)])), pack, extra, layers, sems)


def late_kernel(place, first, second, turn, turn_other, two, before, layers, sems):
    core, quarter, way = (place[k] for k in (2, 3, 4))
    pieces = []
    for k in (0, 1):
        pieces.append((first, 2 + 3 * k, 0, 1 - k, quarter + way))
        pieces.append((second, 2 + 3 * k, 1, 1 - k, quarter + 2 * (1 - core)))
        pieces.append((two.at[k], 0, 0, k, quarter + 2))
        pieces.append((turn.at[k], 0, 1, k, quarter - way))
        pieces.append((turn_other.at[k], 0, 1, 1 - k, quarter + way))
    assemble(place, pieces, (1 - core, (first, second)), None, (), layers, sems)


CHUNK = 256


def forward_one(slot, current, layers, slope, left):
    hidden = current[...]
    left[slot] = lax.dot_general(
        layers[slot, D:], hidden, (((1,), (1,)), ((), ())), preferred_element_type=jnp.float32
    )
    for start in range(0, D, CHUNK):
        cols = slice(start, start + CHUNK)
        preact = jnp.dot(hidden, layers[slot, :D, cols], preferred_element_type=jnp.float32)
        sig = jax.nn.sigmoid(preact)
        slope[slot, :, cols] = sig * (1.0 + preact * (1.0 - sig))
        current[:, cols] = (hidden[:, cols].astype(jnp.float32) + preact * sig).astype(jnp.bfloat16)


def backward_one(slot, current, layers, slope, right):
    upstream = current[...].astype(jnp.float32)
    grad = (upstream * slope[slot]).astype(jnp.bfloat16)
    nt = (((1,), (1,)), ((), ()))
    right[slot] = lax.dot_general(grad, layers[slot, D:], nt, preferred_element_type=jnp.float32)
    for start in range(0, D, CHUNK):
        cols = slice(start, start + CHUNK)
        carried = lax.dot_general(
            grad, layers[slot, cols], nt, preferred_element_type=jnp.float32
        )
        current[:, cols] = (upstream[:, cols] + carried).astype(jnp.bfloat16)


def finish(left, right, factor):
    for slot in range(STAGE):
        product = jnp.dot(
            left[slot],
            right[slot],
            precision=lax.Precision.HIGHEST,
            preferred_element_type=jnp.float32,
        )
        product = product[:RANK, RANK:].astype(jnp.bfloat16)
        factor[slot] = jnp.concatenate([product[: RANK // 2], product[RANK // 2 :]], axis=1)


def rows_of(arrived):
    return arrived[...].reshape(D, TOK).T


def first_kernel(place, arrived, layers, current, slope_out, left, slope, sems):
    def keep(slot):
        return pltpu.make_async_copy(slope.at[slot], slope_out.at[slot], sems.at[slot])

    @pl.when(place[5] == 0)
    def _():
        current[...] = rows_of(arrived)

        def body(slot, carry):
            forward_one(slot, current, layers, slope, left)
            keep(slot).start()
            return carry

        lax.fori_loop(0, STAGE, body, 0)
        for slot in range(STAGE):
            keep(slot).wait()


def middle_kernel(place, hidden, arrived, layers, upstream, factor, current, slope, left, right):
    @pl.when(place[5] == 1)
    def _():
        current[...] = hidden[...]
        upstream[...] = rows_of(arrived)

        def ahead(slot, carry):
            forward_one(slot, current, layers, slope, left)
            return carry

        lax.fori_loop(0, STAGE, ahead, 0)

        def back(step, carry):
            backward_one(STAGE - 1 - step, upstream, layers, slope, right)
            return carry

        lax.fori_loop(0, STAGE, back, 0)
        finish(left, right, factor)


def last_kernel(place, upstream, slope_in, left, late, layers_in, factor, current, slope, right, layers, sems):
    def fetch(slot):
        return (
            pltpu.make_async_copy(slope_in.at[slot], slope.at[slot], sems.at[0, slot]),
            pltpu.make_async_copy(layers_in.at[slot], layers.at[slot], sems.at[1, slot]),
        )

    @pl.when(place[5] == 0)
    def _():
        for slot in reversed(range(STAGE)):
            for copy in fetch(slot):
                copy.start()
        current[...] = upstream[...]

        def back(step, carry):
            slot = STAGE - 1 - step
            for copy in fetch(slot):
                copy.wait()
            backward_one(slot, current, layers, slope, right)
            return carry

        lax.fori_loop(0, STAGE, back, 0)
        finish(left, right, factor)

    @pl.when(place[5] == 1)
    def _():
        factor[...] = late[...]


VMEM = pl.BlockSpec(memory_space=pltpu.VMEM)
SMEM = pl.BlockSpec(memory_space=pltpu.SMEM)
ANY = pl.BlockSpec(memory_space=pl.ANY)
HBM = pl.BlockSpec(memory_space=pltpu.HBM)
PARAMS = pltpu.CompilerParams(vmem_limit_bytes=8 * 1024 * 1024)
SMALL = pltpu.CompilerParams(vmem_limit_bytes=2 * 1024 * 1024)
LARGE = pltpu.CompilerParams(vmem_limit_bytes=30 * 1024 * 1024)
TOKENS = jax.ShapeDtypeStruct((TOK, D), jnp.bfloat16)
SLOPE = jax.ShapeDtypeStruct((STAGE, TOK, D), jnp.float32)
LEFT = jax.ShapeDtypeStruct((STAGE, 2 * RANK, TOK), jnp.float32)
RIGHT = jax.ShapeDtypeStruct((STAGE, TOK, 2 * RANK), jnp.float32)
FACTOR = jax.ShapeDtypeStruct((STAGE, RANK // 2, 2 * RANK), jnp.bfloat16)
LAYERS = jax.ShapeDtypeStruct((STAGE, PACK, D), jnp.bfloat16)
BUNDLE = jax.ShapeDtypeStruct((8, PIECE, D), jnp.bfloat16)


def scratch(shape):
    return pltpu.VMEM(shape.shape, shape.dtype)


def in_hbm(value):
    return pltpu.with_memory_space_constraint(value, pltpu.HBM)


def cost(passes):
    return pl.CostEstimate(
        flops=2 * passes * STAGE * TOK * D * PACK,
        bytes_accessed=STAGE * D * PACK * 2,
        transcendentals=STAGE * TOK * D,
    )


def on_device(inputs, cotangent, weights, proj_in, proj_out, query_factors):
    section, dp = lax.axis_index("section"), lax.axis_index("dp")
    y, col = section // 2, section % 2
    x_hi, z, core = dp // 16, dp // 2 % 8, dp % 2
    stage = y // 4
    quarter = (z + 2 * x_hi) % 4
    way = 1 - 2 * (core ^ x_hi)
    place = jnp.stack([y % 4, col, core, quarter, way, stage]).astype(jnp.int32)

    pack = jnp.concatenate([weights[0], proj_in[0].T, proj_out[0].T])
    rows, beside = gather_rows(pack, core, quarter)

    ahead, seeds = (
        value.reshape(2, 4, TOK, -1).transpose(0, 1, 3, 2).reshape(STAGE, -1, TOK)
        for value in (inputs, cotangent)
    )
    order = [ahead, seeds[4:], seeds[:4]]
    rows[0], order = lax.optimization_barrier((rows[0], jnp.concatenate(order)))
    arrived = lax.all_to_all(order, "section", 0, 0, tiled=True)

    own = jnp.stack(rows)
    own = jnp.stack([own, swap_core(own)])
    queries = query_factors
    queries = jnp.concatenate([queries, swap_core(queries)])
    own, beside, queries = lax.optimization_barrier((own, beside, queries))
    up, side = along_z(own), along_x(own)
    up, side, arrived = lax.optimization_barrier((up, side, arrived))
    turn, two = along_x(up), along_z(up)
    layers, first, second = pl.pallas_call(
        early_kernel,
        out_shape=(LAYERS, BUNDLE, BUNDLE),
        in_specs=[SMEM] + [ANY] * 5,
        out_specs=(VMEM, ANY, ANY),
        scratch_shapes=[pltpu.SemaphoreType.DMA((27,))],
        compiler_params=SMALL,
        cost_estimate=cost(1),
        name="place_early_pieces",
    )(
        place,
        pack,
        in_hbm(beside.reshape(4, PIECE, D)),
        in_hbm(own),
        in_hbm(up.reshape(6, PIECE, D)),
        in_hbm(side.reshape(6, PIECE, D)),
    )
    first, second = swap_core(first), swap_core(second)
    turn, two = lax.optimization_barrier((turn, two))
    turn_other = swap_core(turn)
    layers = pl.pallas_call(
        late_kernel,
        out_shape=LAYERS,
        in_specs=[SMEM] + [ANY] * 5 + [VMEM],
        out_specs=VMEM,
        scratch_shapes=[pltpu.SemaphoreType.DMA((34,))],
        input_output_aliases={6: 0},
        compiler_params=SMALL,
        name="place_late_pieces",
    )(place, first, second, in_hbm(turn), turn_other, in_hbm(two), layers)

    hidden, slope, left = pl.pallas_call(
        first_kernel,
        out_shape=(TOKENS, SLOPE, LEFT),
        in_specs=[SMEM, VMEM, VMEM],
        out_specs=(VMEM, HBM, VMEM),
        scratch_shapes=[scratch(SLOPE), pltpu.SemaphoreType.DMA((STAGE,))],
        compiler_params=PARAMS,
        cost_estimate=cost(1),
        name="forward_first_stage",
    )(place, arrived, layers)
    hidden = move(hidden, lambda x, y, z, c: (x, (y + 2 if y > 1 else y + 6), z, c) if y < 4 else None)
    left, queries = lax.optimization_barrier((left, queries))
    queries = jnp.concatenate([queries, move(queries, lambda x, y, z, c: (x ^ 2, y, z, c))])
    upstream, factor_late = pl.pallas_call(
        middle_kernel,
        out_shape=(TOKENS, FACTOR),
        in_specs=[SMEM, VMEM, VMEM, VMEM],
        out_specs=(VMEM, VMEM),
        scratch_shapes=[scratch(TOKENS), scratch(SLOPE), scratch(LEFT), scratch(RIGHT)],
        compiler_params=PARAMS,
        cost_estimate=cost(2),
        name="second_stage",
    )(place, hidden, arrived, layers)
    upstream = move(upstream, lambda x, y, z, c: (x, (y - 2 if y < 6 else y - 6), z, c) if y > 3 else None)
    upstream, queries = lax.optimization_barrier((upstream, queries))
    factor = pl.pallas_call(
        last_kernel,
        out_shape=FACTOR,
        in_specs=[SMEM, VMEM, HBM, VMEM, VMEM, HBM],
        out_specs=VMEM,
        scratch_shapes=[
            scratch(TOKENS),
            scratch(SLOPE),
            scratch(RIGHT),
            scratch(LAYERS),
            pltpu.SemaphoreType.DMA((2, STAGE)),
        ],
        compiler_params=LARGE,
        cost_estimate=cost(1),
        name="backward_first_stage",
    )(place, upstream, slope, left, factor_late, in_hbm(layers))

    groups = [list(range(8)), list(range(8, 16))]
    parts = lax.all_to_all(factor, "section", 0, 0, tiled=True, axis_index_groups=groups)
    low, high = parts.reshape(2, 4, RANK // 2, 2 * RANK).astype(jnp.float32).sum(1)
    along = [[(h * 8 + k) * 2 + c for k in range(8)] for h in range(2) for c in range(2)]
    sums = jnp.stack([jnp.where(stage == 0, low, high), jnp.where(stage == 0, high, low)])
    sums = sums.astype(jnp.bfloat16)
    sums = lax.all_to_all(
        jnp.broadcast_to(sums[None], (8,) + sums.shape),
        "dp",
        0,
        0,
        tiled=True,
        axis_index_groups=along,
    ).reshape(16, RANK // 2, 2, RANK)
    sums = sums.transpose(0, 2, 1, 3).reshape(16, -1)
    table = lax.dot_general(
        sums, queries.reshape(-1, sums.shape[1]), (((1,), (1,)), ((), ())),
        preferred_element_type=jnp.float32,
    ).reshape(16, 2, 2, -1)
    table = jnp.where(x_hi == 0, table, table[:, ::-1])
    table = jnp.where(core == 0, table, table[:, :, ::-1]).reshape(8, 2, -1)

    outgoing = lax.dynamic_update_slice_in_dim(
        jnp.zeros((16,) + table.shape[1:], jnp.float32), table, x_hi * 8, 0
    )
    scores = lax.all_to_all(outgoing, "section", 0, 0, tiled=True).sum(0)
    scores = scores.reshape(2, 2, 2, -1).transpose(1, 2, 0, 3)

    def part(far, other):
        value = jnp.where((x_hi ^ far) == 0, scores[0], scores[1])
        return jnp.where((core ^ other) == 0, value[0], value[1])

    def send(far, other):
        def target(x, y, z, c):
            holder = x // 2 == (y % 8 * 2 + x % 2) // 8
            return (x ^ 2 if far else x, y, z, c ^ other) if holder else None

        return move(part(far, other), target)

    near, across, diagonal = send(0, 1), send(1, 0), send(1, 1)
    holds = x_hi == section // 8
    mine = jnp.where(holds, part(0, 0), across)
    theirs = jnp.where(holds, near, diagonal)
    return jnp.where(core == 0, jnp.concatenate([mine, theirs]), jnp.concatenate([theirs, mine]))


def solution(mesh):
    placed = (
        P("dp", None, "section"),
        P("dp", None, "section"),
        P("section", None, None),
        P("section", None, None),
        P("section", None, None),
        P("section", "dp", None),
    )
    return jax.shard_map(
        on_device, mesh=mesh, in_specs=placed, out_specs=P("section", "dp"), check_vma=False
    )
```

```python
import functools

import jax
import jax.numpy as jnp
from jax import lax
from jax.experimental import pallas as pl
from jax.experimental.pallas import tpu as pltpu
from jax.sharding import PartitionSpec as P

AXES = ("section", "dp")
TOK = 128
STAGE = 8
D = 1024
RANK = 64
PACK = D + 2 * RANK
PIECE = PACK // 8


def flat(x, y, z, c):
    return (y % 8 * 2 + x % 2) * 32 + ((x % 4 // 2) * 8 + z % 8) * 2 + c


def pairs(target):
    out = []
    for x in range(4):
        for y in range(8):
            for z in range(8):
                for c in range(2):
                    to = target(x, y, z, c)
                    if to is not None:
                        out.append((flat(x, y, z, c), flat(*to)))
    return out


def move(value, target):
    return lax.ppermute(value, AXES, pairs(target))


def swap_core(value):
    return move(value, lambda x, y, z, c: (x, y, z, 1 - c))


def gather_rows(pack, core, quarter):
    piece = lax.dynamic_slice_in_dim(pack, (core * 4 + quarter) * PIECE, PIECE, 0)
    rows = [
        move(piece, lambda x, y, z, c, r=r: (x, y // 4 * 4 + (y + r) % 4, z, c)) for r in (1, 2, 3)
    ]
    half = lax.dynamic_slice_in_dim(pack, core * (PACK // 2), PACK // 2, 0)
    beside = move(half, lambda x, y, z, c: (x + 1 if c == 0 else x - 1, y, z, c))
    return rows, beside


def along_z(value):
    return move(value, lambda x, y, z, c: (x, y, z + 1 - 2 * (c ^ (x // 2)), c))


def along_x(value):
    return move(value, lambda x, y, z, c: (x ^ 1 if c == 0 else 3 - x, y, z, c))


def assemble(place, pieces, beside, whole, extra, layers, sems):
    row, col, core = (place[k] for k in range(3))
    copies = []

    def put(source, target):
        copies.append(pltpu.make_async_copy(source, target, sems.at[len(copies)]))

    def rows(piece):
        return pl.ds(pl.multiple_of(piece * PIECE, PIECE), PIECE)

    if whole is not None:
        put(whole, layers.at[row * 2 + col])
    half, refs = beside
    for k in range(4):
        put(refs[k // 2].at[k % 2], layers.at[row * 2 + 1 - col, rows(half * 4 + k)])
    for distance in (1, 2, 3):
        source_row = (row - distance) & 3
        for ref, index, other_col, other_core, quarter in pieces:
            slot = source_row * 2 + (1 - col if other_col else col)
            half = 1 - core if other_core else core
            put(ref.at[index + distance - 1], layers.at[slot, rows(half * 4 + (quarter & 3))])
    for source, target in extra:
        put(source, target)
    for copy in copies:
        copy.start()
    for copy in copies:
        copy.wait()


def early_kernel(place, pack, beside, own, up, side, layers, first, second, sems):
    core, quarter, way = (place[k] for k in (2, 3, 4))
    pieces = []
    for k in (0, 1):
        pieces.append((own.at[k], 0, 0, k, quarter))
        pieces.append((up, 3 * k, 0, k, quarter - way))
        pieces.append((side, 3 * k, 1, k, quarter + 2 * core))
    extra = [
        (beside.at[pl.ds(0, 2)], first.at[pl.ds(0, 2)]),
        (beside.at[pl.ds(2, 2)], second.at[pl.ds(0, 2)]),
        (up, first.at[pl.ds(2, 6)]),
        (side, second.at[pl.ds(2, 6)]),
    ]
    assemble(place, pieces, (core, (beside.at[pl.ds(0, 2)], beside.at[pl.ds(2, 2)])), pack, extra, layers, sems)


def late_kernel(place, first, second, turn, turn_other, two, before, layers, sems):
    core, quarter, way = (place[k] for k in (2, 3, 4))
    pieces = []
    for k in (0, 1):
        pieces.append((first, 2 + 3 * k, 0, 1 - k, quarter + way))
        pieces.append((second, 2 + 3 * k, 1, 1 - k, quarter + 2 * (1 - core)))
        pieces.append((two.at[k], 0, 0, k, quarter + 2))
        pieces.append((turn.at[k], 0, 1, k, quarter - way))
        pieces.append((turn_other.at[k], 0, 1, 1 - k, quarter + way))
    assemble(place, pieces, (1 - core, (first, second)), None, (), layers, sems)


CHUNK = 256


def forward_one(slot, current, layers, slope, left):
    hidden = current[...]
    left[slot] = lax.dot_general(
        layers[slot, D:], hidden, (((1,), (1,)), ((), ())), preferred_element_type=jnp.float32
    )
    for start in range(0, D, CHUNK):
        cols = slice(start, start + CHUNK)
        preact = jnp.dot(hidden, layers[slot, :D, cols], preferred_element_type=jnp.float32)
        sig = jax.nn.sigmoid(preact)
        slope[slot, :, cols] = sig * (1.0 + preact * (1.0 - sig))
        current[:, cols] = (hidden[:, cols].astype(jnp.float32) + preact * sig).astype(jnp.bfloat16)


def backward_one(slot, current, layers, slope, right):
    upstream = current[...].astype(jnp.float32)
    grad = (upstream * slope[slot]).astype(jnp.bfloat16)
    nt = (((1,), (1,)), ((), ()))
    right[slot] = lax.dot_general(grad, layers[slot, D:], nt, preferred_element_type=jnp.float32)
    for start in range(0, D, CHUNK):
        cols = slice(start, start + CHUNK)
        carried = lax.dot_general(
            grad, layers[slot, cols], nt, preferred_element_type=jnp.float32
        )
        current[:, cols] = (upstream[:, cols] + carried).astype(jnp.bfloat16)


def finish(left, right, factor):
    for slot in range(STAGE):
        product = jnp.dot(
            left[slot],
            right[slot],
            precision=lax.Precision.HIGHEST,
            preferred_element_type=jnp.float32,
        )
        product = product[:RANK, RANK:].astype(jnp.bfloat16)
        factor[slot] = jnp.concatenate([product[: RANK // 2], product[RANK // 2 :]], axis=1)


def rows_of(arrived):
    return arrived[...].reshape(D, TOK).T


def first_kernel(place, arrived, layers, current, slope_out, left, slope, sems):
    def keep(slot):
        return pltpu.make_async_copy(slope.at[slot], slope_out.at[slot], sems.at[slot])

    @pl.when(place[5] == 0)
    def _():
        current[...] = rows_of(arrived)

        def body(slot, carry):
            forward_one(slot, current, layers, slope, left)
            keep(slot).start()
            return carry

        lax.fori_loop(0, STAGE, body, 0)
        for slot in range(STAGE):
            keep(slot).wait()


def middle_kernel(place, hidden, arrived, layers, upstream, factor, current, slope, left, right):
    @pl.when(place[5] == 1)
    def _():
        current[...] = hidden[...]
        upstream[...] = rows_of(arrived)

        def ahead(slot, carry):
            forward_one(slot, current, layers, slope, left)
            return carry

        lax.fori_loop(0, STAGE, ahead, 0)

        def back(step, carry):
            backward_one(STAGE - 1 - step, upstream, layers, slope, right)
            return carry

        lax.fori_loop(0, STAGE, back, 0)
        finish(left, right, factor)


def last_kernel(place, upstream, slope_in, left, late, layers_in, factor, current, slope, right, layers, sems):
    def fetch(slot):
        return (
            pltpu.make_async_copy(slope_in.at[slot], slope.at[slot], sems.at[0, slot]),
            pltpu.make_async_copy(layers_in.at[slot], layers.at[slot], sems.at[1, slot]),
        )

    @pl.when(place[5] == 0)
    def _():
        for slot in reversed(range(STAGE)):
            for copy in fetch(slot):
                copy.start()
        current[...] = upstream[...]

        def back(step, carry):
            slot = STAGE - 1 - step
            for copy in fetch(slot):
                copy.wait()
            backward_one(slot, current, layers, slope, right)
            return carry

        lax.fori_loop(0, STAGE, back, 0)
        finish(left, right, factor)

    @pl.when(place[5] == 1)
    def _():
        factor[...] = late[...]


VMEM = pl.BlockSpec(memory_space=pltpu.VMEM)
SMEM = pl.BlockSpec(memory_space=pltpu.SMEM)
ANY = pl.BlockSpec(memory_space=pl.ANY)
HBM = pl.BlockSpec(memory_space=pltpu.HBM)
PARAMS = pltpu.CompilerParams(vmem_limit_bytes=8 * 1024 * 1024)
SMALL = pltpu.CompilerParams(vmem_limit_bytes=2 * 1024 * 1024)
LARGE = pltpu.CompilerParams(vmem_limit_bytes=30 * 1024 * 1024)
TOKENS = jax.ShapeDtypeStruct((TOK, D), jnp.bfloat16)
SLOPE = jax.ShapeDtypeStruct((STAGE, TOK, D), jnp.float32)
LEFT = jax.ShapeDtypeStruct((STAGE, 2 * RANK, TOK), jnp.float32)
RIGHT = jax.ShapeDtypeStruct((STAGE, TOK, 2 * RANK), jnp.float32)
FACTOR = jax.ShapeDtypeStruct((STAGE, RANK // 2, 2 * RANK), jnp.bfloat16)
LAYERS = jax.ShapeDtypeStruct((STAGE, PACK, D), jnp.bfloat16)
BUNDLE = jax.ShapeDtypeStruct((8, PIECE, D), jnp.bfloat16)


def scratch(shape):
    return pltpu.VMEM(shape.shape, shape.dtype)


def in_hbm(value):
    return pltpu.with_memory_space_constraint(value, pltpu.HBM)


def cost(passes):
    return pl.CostEstimate(
        flops=2 * passes * STAGE * TOK * D * PACK,
        bytes_accessed=STAGE * D * PACK * 2,
        transcendentals=STAGE * TOK * D,
    )


def on_device(inputs, cotangent, weights, proj_in, proj_out, query_factors):
    section, dp = lax.axis_index("section"), lax.axis_index("dp")
    y, col = section // 2, section % 2
    x_hi, z, core = dp // 16, dp // 2 % 8, dp % 2
    stage = y // 4
    quarter = (z + 2 * x_hi) % 4
    way = 1 - 2 * (core ^ x_hi)
    place = jnp.stack([y % 4, col, core, quarter, way, stage]).astype(jnp.int32)

    pack = jnp.concatenate([weights[0], proj_in[0].T, proj_out[0].T])
    rows, beside = gather_rows(pack, core, quarter)

    ahead, seeds = (
        value.reshape(2, 4, TOK, -1).transpose(0, 1, 3, 2).reshape(STAGE, -1, TOK)
        for value in (inputs, cotangent)
    )
    order = [ahead, seeds[4:], seeds[:4]]
    rows[0], order = lax.optimization_barrier((rows[0], jnp.concatenate(order)))
    arrived = lax.all_to_all(order, "section", 0, 0, tiled=True)

    own = jnp.stack(rows)
    own = jnp.stack([own, swap_core(own)])
    queries = query_factors
    queries = jnp.concatenate([queries, swap_core(queries)])
    own, beside, queries = lax.optimization_barrier((own, beside, queries))
    up, side = along_z(own), along_x(own)
    up, side, arrived = lax.optimization_barrier((up, side, arrived))
    turn, two = along_x(up), along_z(up)
    layers, first, second = pl.pallas_call(
        early_kernel,
        out_shape=(LAYERS, BUNDLE, BUNDLE),
        in_specs=[SMEM] + [ANY] * 5,
        out_specs=(VMEM, ANY, ANY),
        scratch_shapes=[pltpu.SemaphoreType.DMA((27,))],
        compiler_params=SMALL,
        cost_estimate=cost(1),
        name="place_early_pieces",
    )(
        place,
        pack,
        in_hbm(beside.reshape(4, PIECE, D)),
        in_hbm(own),
        in_hbm(up.reshape(6, PIECE, D)),
        in_hbm(side.reshape(6, PIECE, D)),
    )
    first, second = swap_core(first), swap_core(second)
    turn, two = lax.optimization_barrier((turn, two))
    turn_other = swap_core(turn)
    layers = pl.pallas_call(
        late_kernel,
        out_shape=LAYERS,
        in_specs=[SMEM] + [ANY] * 5 + [VMEM],
        out_specs=VMEM,
        scratch_shapes=[pltpu.SemaphoreType.DMA((34,))],
        input_output_aliases={6: 0},
        compiler_params=SMALL,
        name="place_late_pieces",
    )(place, first, second, in_hbm(turn), turn_other, in_hbm(two), layers)

    hidden, slope, left = pl.pallas_call(
        first_kernel,
        out_shape=(TOKENS, SLOPE, LEFT),
        in_specs=[SMEM, VMEM, VMEM],
        out_specs=(VMEM, HBM, VMEM),
        scratch_shapes=[scratch(SLOPE), pltpu.SemaphoreType.DMA((STAGE,))],
        compiler_params=PARAMS,
        cost_estimate=cost(1),
        name="forward_first_stage",
    )(place, arrived, layers)
    hidden = move(hidden, lambda x, y, z, c: (x, (y + 2 if y > 1 else y + 6), z, c) if y < 4 else None)
    left, queries = lax.optimization_barrier((left, queries))
    queries = jnp.concatenate([queries, move(queries, lambda x, y, z, c: (x ^ 2, y, z, c))])
    upstream, factor_late = pl.pallas_call(
        middle_kernel,
        out_shape=(TOKENS, FACTOR),
        in_specs=[SMEM, VMEM, VMEM, VMEM],
        out_specs=(VMEM, VMEM),
        scratch_shapes=[scratch(TOKENS), scratch(SLOPE), scratch(LEFT), scratch(RIGHT)],
        compiler_params=PARAMS,
        cost_estimate=cost(2),
        name="second_stage",
    )(place, hidden, arrived, layers)
    upstream = move(upstream, lambda x, y, z, c: (x, (y - 2 if y < 6 else y - 6), z, c) if y > 3 else None)
    upstream, queries = lax.optimization_barrier((upstream, queries))
    factor = pl.pallas_call(
        last_kernel,
        out_shape=FACTOR,
        in_specs=[SMEM, VMEM, HBM, VMEM, VMEM, HBM],
        out_specs=VMEM,
        scratch_shapes=[
            scratch(TOKENS),
            scratch(SLOPE),
            scratch(RIGHT),
            scratch(LAYERS),
            pltpu.SemaphoreType.DMA((2, STAGE)),
        ],
        compiler_params=LARGE,
        cost_estimate=cost(1),
        name="backward_first_stage",
    )(place, upstream, slope, left, factor_late, in_hbm(layers))

    groups = [list(range(8)), list(range(8, 16))]
    parts = lax.all_to_all(factor, "section", 0, 0, tiled=True, axis_index_groups=groups)
    low, high = parts.reshape(2, 4, RANK // 2, 2 * RANK).astype(jnp.float32).sum(1)
    along = [[(h * 8 + k) * 2 + c for k in range(8)] for h in range(2) for c in range(2)]
    sums = jnp.stack([jnp.where(stage == 0, low, high), jnp.where(stage == 0, high, low)])
    sums = sums.astype(jnp.bfloat16)
    sums = lax.all_to_all(
        jnp.broadcast_to(sums[None], (8,) + sums.shape),
        "dp",
        0,
        0,
        tiled=True,
        axis_index_groups=along,
    ).reshape(16, RANK // 2, 2, RANK)
    sums = sums.transpose(0, 2, 1, 3).reshape(16, -1)
    table = lax.dot_general(
        sums, queries.reshape(-1, sums.shape[1]), (((1,), (1,)), ((), ())),
        preferred_element_type=jnp.float32,
    ).reshape(16, 2, 2, -1)
    table = jnp.where(x_hi == 0, table, table[:, ::-1])
    table = jnp.where(core == 0, table, table[:, :, ::-1]).reshape(8, 2, -1)

    table = table.reshape(8, 2, 4, -1).transpose(0, 2, 1, 3)
    outgoing = lax.dynamic_update_slice_in_dim(
        jnp.zeros((16,) + table.shape[1:], jnp.float32), table, x_hi * 8, 0
    ).reshape(64, -1)
    plane = [
        [s * 32 + (h * 8 + k) * 2 + c for s in range(16) for h in range(2) for c in range(2)]
        for k in range(8)
    ]
    scores = lax.all_to_all(outgoing, AXES, 0, 0, tiled=True, axis_index_groups=plane)
    return scores.reshape(32, 4, -1).sum(0).reshape(4, -1)


def solution(mesh):
    placed = (
        P("dp", None, "section"),
        P("dp", None, "section"),
        P("section", None, None),
        P("section", None, None),
        P("section", None, None),
        P("section", "dp", None),
    )
    return jax.shard_map(
        on_device, mesh=mesh, in_specs=placed, out_specs=P("section", "dp"), check_vma=False
    )
```

```python
import functools

import jax
import jax.numpy as jnp
from jax import lax
from jax.experimental import pallas as pl
from jax.experimental.pallas import tpu as pltpu
from jax.sharding import PartitionSpec as P

AXES = ("section", "dp")
TOK = 128
STAGE = 8
D = 1024
RANK = 64
PACK = D + 2 * RANK
PIECE = PACK // 8


def flat(x, y, z, c):
    return (y % 8 * 2 + x % 2) * 32 + ((x % 4 // 2) * 8 + z % 8) * 2 + c


def pairs(target):
    out = []
    for x in range(4):
        for y in range(8):
            for z in range(8):
                for c in range(2):
                    to = target(x, y, z, c)
                    if to is not None:
                        out.append((flat(x, y, z, c), flat(*to)))
    return out


def move(value, target):
    return lax.ppermute(value, AXES, pairs(target))


def swap_core(value):
    return move(value, lambda x, y, z, c: (x, y, z, 1 - c))


def gather_rows(pack, core, quarter):
    piece = lax.dynamic_slice_in_dim(pack, (core * 4 + quarter) * PIECE, PIECE, 0)
    rows = [
        move(piece, lambda x, y, z, c, r=r: (x, y // 4 * 4 + (y + r) % 4, z, c)) for r in (1, 2, 3)
    ]
    half = lax.dynamic_slice_in_dim(pack, core * (PACK // 2), PACK // 2, 0)
    beside = move(half, lambda x, y, z, c: (x + 1 if c == 0 else x - 1, y, z, c))
    return rows, beside


def along_z(value):
    return move(value, lambda x, y, z, c: (x, y, z + 1 - 2 * (c ^ (x // 2)), c))


def along_x(value):
    return move(value, lambda x, y, z, c: (x ^ 1 if c == 0 else 3 - x, y, z, c))


def assemble(place, pieces, beside, whole, extra, layers, sems):
    row, col, core = (place[k] for k in range(3))
    copies = []

    def put(source, target):
        copies.append(pltpu.make_async_copy(source, target, sems.at[len(copies)]))

    def rows(piece):
        return pl.ds(pl.multiple_of(piece * PIECE, PIECE), PIECE)

    if whole is not None:
        put(whole, layers.at[row * 2 + col])
    half, refs = beside
    for k in range(4):
        put(refs[k // 2].at[k % 2], layers.at[row * 2 + 1 - col, rows(half * 4 + k)])
    for distance in (1, 2, 3):
        source_row = (row - distance) & 3
        for ref, index, other_col, other_core, quarter in pieces:
            slot = source_row * 2 + (1 - col if other_col else col)
            half = 1 - core if other_core else core
            put(ref.at[index + distance - 1], layers.at[slot, rows(half * 4 + (quarter & 3))])
    for source, target in extra:
        put(source, target)
    for copy in copies:
        copy.start()
    for copy in copies:
        copy.wait()


def early_kernel(place, pack, beside, own, up, side, layers, first, second, sems):
    core, quarter, way = (place[k] for k in (2, 3, 4))
    pieces = []
    for k in (0, 1):
        pieces.append((own.at[k], 0, 0, k, quarter))
        pieces.append((up, 3 * k, 0, k, quarter - way))
        pieces.append((side, 3 * k, 1, k, quarter + 2 * core))
    extra = [
        (beside.at[pl.ds(0, 2)], first.at[pl.ds(0, 2)]),
        (beside.at[pl.ds(2, 2)], second.at[pl.ds(0, 2)]),
        (up, first.at[pl.ds(2, 6)]),
        (side, second.at[pl.ds(2, 6)]),
    ]
    assemble(place, pieces, (core, (beside.at[pl.ds(0, 2)], beside.at[pl.ds(2, 2)])), pack, extra, layers, sems)


CHUNK = 256


def forward_one(slot, current, layers, slope, left):
    hidden = current[...]
    left[slot] = lax.dot_general(
        layers[slot, D:], hidden, (((1,), (1,)), ((), ())), preferred_element_type=jnp.float32
    )
    for start in range(0, D, CHUNK):
        cols = slice(start, start + CHUNK)
        preact = jnp.dot(hidden, layers[slot, :D, cols], preferred_element_type=jnp.float32)
        sig = jax.nn.sigmoid(preact)
        slope[slot, :, cols] = sig * (1.0 + preact * (1.0 - sig))
        current[:, cols] = (hidden[:, cols].astype(jnp.float32) + preact * sig).astype(jnp.bfloat16)


def backward_one(slot, current, layers, slope, right):
    upstream = current[...].astype(jnp.float32)
    grad = (upstream * slope[slot]).astype(jnp.bfloat16)
    nt = (((1,), (1,)), ((), ()))
    right[slot] = lax.dot_general(grad, layers[slot, D:], nt, preferred_element_type=jnp.float32)
    for start in range(0, D, CHUNK):
        cols = slice(start, start + CHUNK)
        carried = lax.dot_general(
            grad, layers[slot, cols], nt, preferred_element_type=jnp.float32
        )
        current[:, cols] = (upstream[:, cols] + carried).astype(jnp.bfloat16)


def finish(left, right, factor):
    for slot in range(STAGE):
        product = jnp.dot(
            left[slot],
            right[slot],
            precision=lax.Precision.HIGHEST,
            preferred_element_type=jnp.float32,
        )
        product = product[:RANK, RANK:].astype(jnp.bfloat16)
        factor[slot] = jnp.concatenate([product[: RANK // 2], product[RANK // 2 :]], axis=1)


def rows_of(arrived):
    return arrived[...].reshape(D, TOK).T


def first_kernel(
    place, arrived, first, second, turn, turn_other, two, before,
    current, slope_out, left, layers, slope, sems, late_sems
):
    row, col, core, quarter, way = (place[k] for k in range(5))

    def rows(piece):
        return pl.ds(pl.multiple_of(piece * PIECE, PIECE), PIECE)

    pieces = []
    for k in (0, 1):
        pieces.append((first, 2 + 3 * k, 0, 1 - k, quarter + way))
        pieces.append((second, 2 + 3 * k, 1, 1 - k, quarter + 2 * (1 - core)))
        pieces.append((two.at[k], 0, 0, k, quarter + 2))
        pieces.append((turn.at[k], 0, 1, k, quarter - way))
        pieces.append((turn_other.at[k], 0, 1, 1 - k, quarter + way))
    for k in range(4):
        target = layers.at[row * 2 + 1 - col, rows((1 - core) * 4 + k)]
        pltpu.make_async_copy((first, second)[k // 2].at[k % 2], target, late_sems.at[0, k]).start()
    for distance in (1, 2, 3):
        source_row = (row - distance) & 3
        for k, (ref, index, other_col, other_core, which) in enumerate(pieces):
            slot = source_row * 2 + (1 - col if other_col else col)
            half = 1 - core if other_core else core
            target = layers.at[slot, rows(half * 4 + (which & 3))]
            source = ref.at[index + distance - 1]
            pltpu.make_async_copy(source, target, late_sems.at[distance, k]).start()

    def await_row(source_row):
        distance = (row - source_row) & 3

        def done(k):
            target = layers.at[0, pl.ds(0, PIECE)]
            pltpu.make_async_copy(first.at[0], target, late_sems.at[distance, k]).wait()

        for k in range(4):
            done(k)

        @pl.when(distance > 0)
        def _():
            for k in range(4, len(pieces)):
                done(k)

    def keep(slot):
        return pltpu.make_async_copy(slope.at[slot], slope_out.at[slot], sems.at[slot])

    @pl.when(place[5] == 0)
    def _():
        current[...] = rows_of(arrived)

        def body(slot, carry):
            @pl.when((slot & 1) == 0)
            def _():
                await_row(slot >> 1)

            forward_one(slot, current, layers, slope, left)
            keep(slot).start()
            return carry

        lax.fori_loop(0, STAGE, body, 0)
        for slot in range(STAGE):
            keep(slot).wait()

    @pl.when(place[5] == 1)
    def _():
        for source_row in range(4):
            await_row(source_row)


def middle_kernel(place, hidden, arrived, layers, upstream, factor, current, slope, left, right):
    @pl.when(place[5] == 1)
    def _():
        current[...] = hidden[...]
        upstream[...] = rows_of(arrived)

        def ahead(slot, carry):
            forward_one(slot, current, layers, slope, left)
            return carry

        lax.fori_loop(0, STAGE, ahead, 0)

        def back(step, carry):
            backward_one(STAGE - 1 - step, upstream, layers, slope, right)
            return carry

        lax.fori_loop(0, STAGE, back, 0)
        finish(left, right, factor)


def last_kernel(place, upstream, slope_in, left, late, layers_in, factor, current, slope, right, layers, sems):
    def fetch(slot):
        return (
            pltpu.make_async_copy(slope_in.at[slot], slope.at[slot], sems.at[0, slot]),
            pltpu.make_async_copy(layers_in.at[slot], layers.at[slot], sems.at[1, slot]),
        )

    @pl.when(place[5] == 0)
    def _():
        for slot in reversed(range(STAGE)):
            for copy in fetch(slot):
                copy.start()
        current[...] = upstream[...]

        def back(step, carry):
            slot = STAGE - 1 - step
            for copy in fetch(slot):
                copy.wait()
            backward_one(slot, current, layers, slope, right)
            return carry

        lax.fori_loop(0, STAGE, back, 0)
        finish(left, right, factor)

    @pl.when(place[5] == 1)
    def _():
        factor[...] = late[...]


VMEM = pl.BlockSpec(memory_space=pltpu.VMEM)
SMEM = pl.BlockSpec(memory_space=pltpu.SMEM)
ANY = pl.BlockSpec(memory_space=pl.ANY)
HBM = pl.BlockSpec(memory_space=pltpu.HBM)
PARAMS = pltpu.CompilerParams(vmem_limit_bytes=8 * 1024 * 1024)
SMALL = pltpu.CompilerParams(vmem_limit_bytes=2 * 1024 * 1024)
LARGE = pltpu.CompilerParams(vmem_limit_bytes=30 * 1024 * 1024)
TOKENS = jax.ShapeDtypeStruct((TOK, D), jnp.bfloat16)
SLOPE = jax.ShapeDtypeStruct((STAGE, TOK, D), jnp.float32)
LEFT = jax.ShapeDtypeStruct((STAGE, 2 * RANK, TOK), jnp.float32)
RIGHT = jax.ShapeDtypeStruct((STAGE, TOK, 2 * RANK), jnp.float32)
FACTOR = jax.ShapeDtypeStruct((STAGE, RANK // 2, 2 * RANK), jnp.bfloat16)
LAYERS = jax.ShapeDtypeStruct((STAGE, PACK, D), jnp.bfloat16)
BUNDLE = jax.ShapeDtypeStruct((8, PIECE, D), jnp.bfloat16)


def scratch(shape):
    return pltpu.VMEM(shape.shape, shape.dtype)


def in_hbm(value):
    return pltpu.with_memory_space_constraint(value, pltpu.HBM)


def cost(passes):
    return pl.CostEstimate(
        flops=2 * passes * STAGE * TOK * D * PACK,
        bytes_accessed=STAGE * D * PACK * 2,
        transcendentals=STAGE * TOK * D,
    )


def on_device(inputs, cotangent, weights, proj_in, proj_out, query_factors):
    section, dp = lax.axis_index("section"), lax.axis_index("dp")
    y, col = section // 2, section % 2
    x_hi, z, core = dp // 16, dp // 2 % 8, dp % 2
    stage = y // 4
    quarter = (z + 2 * x_hi) % 4
    way = 1 - 2 * (core ^ x_hi)
    place = jnp.stack([y % 4, col, core, quarter, way, stage]).astype(jnp.int32)

    pack = jnp.concatenate([weights[0], proj_in[0].T, proj_out[0].T])
    rows, beside = gather_rows(pack, core, quarter)

    ahead, seeds = (
        value.reshape(2, 4, TOK, -1).transpose(0, 1, 3, 2).reshape(STAGE, -1, TOK)
        for value in (inputs, cotangent)
    )
    order = [ahead, seeds[4:], seeds[:4]]
    rows[0], order = lax.optimization_barrier((rows[0], jnp.concatenate(order)))
    arrived = lax.all_to_all(order, "section", 0, 0, tiled=True)

    own = jnp.stack(rows)
    own = jnp.stack([own, swap_core(own)])
    queries = query_factors
    queries = jnp.concatenate([queries, swap_core(queries)])
    own, beside, queries = lax.optimization_barrier((own, beside, queries))
    up, side = along_z(own), along_x(own)
    up, side, arrived = lax.optimization_barrier((up, side, arrived))
    turn, two = along_x(up), along_z(up)
    layers, first, second = pl.pallas_call(
        early_kernel,
        out_shape=(LAYERS, BUNDLE, BUNDLE),
        in_specs=[SMEM] + [ANY] * 5,
        out_specs=(VMEM, ANY, ANY),
        scratch_shapes=[pltpu.SemaphoreType.DMA((27,))],
        compiler_params=SMALL,
        cost_estimate=cost(1),
        name="place_early_pieces",
    )(
        place,
        pack,
        in_hbm(beside.reshape(4, PIECE, D)),
        in_hbm(own),
        in_hbm(up.reshape(6, PIECE, D)),
        in_hbm(side.reshape(6, PIECE, D)),
    )
    first, second = swap_core(first), swap_core(second)
    turn, two = lax.optimization_barrier((turn, two))
    turn_other = swap_core(turn)
    hidden, slope, left, layers = pl.pallas_call(
        first_kernel,
        out_shape=(TOKENS, SLOPE, LEFT, LAYERS),
        in_specs=[SMEM, VMEM] + [ANY] * 5 + [VMEM],
        out_specs=(VMEM, HBM, VMEM, VMEM),
        scratch_shapes=[
            scratch(SLOPE),
            pltpu.SemaphoreType.DMA((STAGE,)),
            pltpu.SemaphoreType.DMA((4, 10)),
        ],
        input_output_aliases={7: 3},
        compiler_params=PARAMS,
        cost_estimate=cost(1),
        name="forward_first_stage",
    )(place, arrived, first, second, in_hbm(turn), turn_other, in_hbm(two), layers)
    hidden = move(hidden, lambda x, y, z, c: (x, (y + 2 if y > 1 else y + 6), z, c) if y < 4 else None)
    left, queries = lax.optimization_barrier((left, queries))
    queries = jnp.concatenate([queries, move(queries, lambda x, y, z, c: (x ^ 2, y, z, c))])
    upstream, factor_late = pl.pallas_call(
        middle_kernel,
        out_shape=(TOKENS, FACTOR),
        in_specs=[SMEM, VMEM, VMEM, VMEM],
        out_specs=(VMEM, VMEM),
        scratch_shapes=[scratch(TOKENS), scratch(SLOPE), scratch(LEFT), scratch(RIGHT)],
        compiler_params=PARAMS,
        cost_estimate=cost(2),
        name="second_stage",
    )(place, hidden, arrived, layers)
    upstream = move(upstream, lambda x, y, z, c: (x, (y - 2 if y < 6 else y - 6), z, c) if y > 3 else None)
    upstream, queries = lax.optimization_barrier((upstream, queries))
    factor = pl.pallas_call(
        last_kernel,
        out_shape=FACTOR,
        in_specs=[SMEM, VMEM, HBM, VMEM, VMEM, HBM],
        out_specs=VMEM,
        scratch_shapes=[
            scratch(TOKENS),
            scratch(SLOPE),
            scratch(RIGHT),
            scratch(LAYERS),
            pltpu.SemaphoreType.DMA((2, STAGE)),
        ],
        compiler_params=LARGE,
        cost_estimate=cost(1),
        name="backward_first_stage",
    )(place, upstream, slope, left, factor_late, in_hbm(layers))

    groups = [list(range(8)), list(range(8, 16))]
    parts = lax.all_to_all(factor, "section", 0, 0, tiled=True, axis_index_groups=groups)
    low, high = parts.reshape(2, 4, RANK // 2, 2 * RANK).astype(jnp.float32).sum(1)
    along = [[(h * 8 + k) * 2 + c for k in range(8)] for h in range(2) for c in range(2)]
    sums = jnp.stack([jnp.where(stage == 0, low, high), jnp.where(stage == 0, high, low)])
    sums = sums.astype(jnp.bfloat16)
    sums = lax.all_to_all(
        jnp.broadcast_to(sums[None], (8,) + sums.shape),
        "dp",
        0,
        0,
        tiled=True,
        axis_index_groups=along,
    ).reshape(16, RANK // 2, 2, RANK)
    sums = sums.transpose(0, 2, 1, 3).reshape(16, -1)
    table = lax.dot_general(
        sums, queries.reshape(-1, sums.shape[1]), (((1,), (1,)), ((), ())),
        preferred_element_type=jnp.float32,
    ).reshape(16, 2, 2, -1)
    table = jnp.where(x_hi == 0, table, table[:, ::-1])
    table = jnp.where(core == 0, table, table[:, :, ::-1]).reshape(8, 2, -1)

    table = table.reshape(8, 2, 4, -1).transpose(0, 2, 1, 3)
    outgoing = lax.dynamic_update_slice_in_dim(
        jnp.zeros((16,) + table.shape[1:], jnp.float32), table, x_hi * 8, 0
    ).reshape(64, -1)
    plane = [
        [s * 32 + (h * 8 + k) * 2 + c for s in range(16) for h in range(2) for c in range(2)]
        for k in range(8)
    ]
    scores = lax.all_to_all(outgoing, AXES, 0, 0, tiled=True, axis_index_groups=plane)
    return scores.reshape(32, 4, -1).sum(0).reshape(4, -1)


def solution(mesh):
    placed = (
        P("dp", None, "section"),
        P("dp", None, "section"),
        P("section", None, None),
        P("section", None, None),
        P("section", None, None),
        P("section", "dp", None),
    )
    return jax.shard_map(
        on_device, mesh=mesh, in_specs=placed, out_specs=P("section", "dp"), check_vma=False
    )
```

```python
import functools

import jax
import jax.numpy as jnp
from jax import lax
from jax.experimental import pallas as pl
from jax.experimental.pallas import tpu as pltpu
from jax.sharding import PartitionSpec as P

AXES = ("section", "dp")
TOK = 128
STAGE = 8
D = 1024
RANK = 64
PACK = D + 2 * RANK
PIECE = PACK // 8


def flat(x, y, z, c):
    return (y % 8 * 2 + x % 2) * 32 + ((x % 4 // 2) * 8 + z % 8) * 2 + c


def pairs(target):
    out = []
    for x in range(4):
        for y in range(8):
            for z in range(8):
                for c in range(2):
                    to = target(x, y, z, c)
                    if to is not None:
                        out.append((flat(x, y, z, c), flat(*to)))
    return out


def move(value, target):
    return lax.ppermute(value, AXES, pairs(target))


def swap_core(value):
    return move(value, lambda x, y, z, c: (x, y, z, 1 - c))


def gather_rows(pack, core, quarter):
    piece = lax.dynamic_slice_in_dim(pack, (core * 4 + quarter) * PIECE, PIECE, 0)
    rows = [
        move(piece, lambda x, y, z, c, r=r: (x, y // 4 * 4 + (y + r) % 4, z, c)) for r in (1, 2, 3)
    ]
    half = lax.dynamic_slice_in_dim(pack, core * (PACK // 2), PACK // 2, 0)
    beside = move(half, lambda x, y, z, c: (x + 1 if c == 0 else x - 1, y, z, c))
    return rows, beside


def along_z(value):
    return move(value, lambda x, y, z, c: (x, y, z + 1 - 2 * (c ^ (x // 2)), c))


def along_x(value):
    return move(value, lambda x, y, z, c: (x ^ 1 if c == 0 else 3 - x, y, z, c))


def assemble(place, pieces, beside, whole, extra, layers, sems):
    row, col, core = (place[k] for k in range(3))
    copies = []

    def put(source, target):
        copies.append(pltpu.make_async_copy(source, target, sems.at[len(copies)]))

    def rows(piece):
        return pl.ds(pl.multiple_of(piece * PIECE, PIECE), PIECE)

    if whole is not None:
        put(whole, layers.at[row * 2 + col])
    half, refs = beside
    for k in range(4):
        put(refs[k // 2].at[k % 2], layers.at[row * 2 + 1 - col, rows(half * 4 + k)])
    for distance in (1, 2, 3):
        source_row = (row - distance) & 3
        for ref, index, other_col, other_core, quarter in pieces:
            slot = source_row * 2 + (1 - col if other_col else col)
            half = 1 - core if other_core else core
            put(ref.at[index + distance - 1], layers.at[slot, rows(half * 4 + (quarter & 3))])
    for source, target in extra:
        put(source, target)
    for copy in copies:
        copy.start()
    for copy in copies:
        copy.wait()


def early_kernel(place, pack, beside, own, up, side, layers, first, second, sems):
    core, quarter, way = (place[k] for k in (2, 3, 4))
    pieces = []
    for k in (0, 1):
        pieces.append((own.at[k], 0, 0, k, quarter))
        pieces.append((up, 3 * k, 0, k, quarter - way))
        pieces.append((side, 3 * k, 1, k, quarter + 2 * core))
    extra = [
        (beside.at[pl.ds(0, 2)], first.at[pl.ds(0, 2)]),
        (beside.at[pl.ds(2, 2)], second.at[pl.ds(0, 2)]),
        (up, first.at[pl.ds(2, 6)]),
        (side, second.at[pl.ds(2, 6)]),
    ]
    assemble(place, pieces, (core, (beside.at[pl.ds(0, 2)], beside.at[pl.ds(2, 2)])), pack, extra, layers, sems)


CHUNK = 256


def forward_one(slot, current, layers, slope, left):
    hidden = current[...]
    left[slot] = lax.dot_general(
        layers[slot, D:], hidden, (((1,), (1,)), ((), ())), preferred_element_type=jnp.float32
    )
    for start in range(0, D, CHUNK):
        cols = slice(start, start + CHUNK)
        preact = jnp.dot(hidden, layers[slot, :D, cols], preferred_element_type=jnp.float32)
        sig = jax.nn.sigmoid(preact)
        slope[slot, :, cols] = sig * (1.0 + preact * (1.0 - sig))
        current[:, cols] = (hidden[:, cols].astype(jnp.float32) + preact * sig).astype(jnp.bfloat16)


def backward_one(slot, current, layers, slope, right):
    upstream = current[...].astype(jnp.float32)
    grad = (upstream * slope[slot]).astype(jnp.bfloat16)
    nt = (((1,), (1,)), ((), ()))
    right[slot] = lax.dot_general(grad, layers[slot, D:], nt, preferred_element_type=jnp.float32)
    for start in range(0, D, CHUNK // 2):
        cols = slice(start, start + CHUNK // 2)
        carried = lax.dot_general(
            grad, layers[slot, cols], nt, preferred_element_type=jnp.float32
        )
        current[:, cols] = (upstream[:, cols] + carried).astype(jnp.bfloat16)


def finish(left, right, factor):
    for slot in range(STAGE):
        product = jnp.dot(
            left[slot],
            right[slot],
            precision=lax.Precision.HIGHEST,
            preferred_element_type=jnp.float32,
        )
        product = product[:RANK, RANK:].astype(jnp.bfloat16)
        factor[slot] = jnp.concatenate([product[: RANK // 2], product[RANK // 2 :]], axis=1)


def rows_of(arrived):
    return arrived[...].reshape(D, TOK).T


def first_kernel(
    place, arrived, first, second, turn, turn_other, two, before,
    current, slope_out, left, layers, slope, sems, late_sems
):
    row, col, core, quarter, way = (place[k] for k in range(5))

    def rows(piece):
        return pl.ds(pl.multiple_of(piece * PIECE, PIECE), PIECE)

    pieces = []
    for k in (0, 1):
        pieces.append((first, 2 + 3 * k, 0, 1 - k, quarter + way))
        pieces.append((second, 2 + 3 * k, 1, 1 - k, quarter + 2 * (1 - core)))
        pieces.append((two.at[k], 0, 0, k, quarter + 2))
        pieces.append((turn.at[k], 0, 1, k, quarter - way))
        pieces.append((turn_other.at[k], 0, 1, 1 - k, quarter + way))
    for k in range(4):
        target = layers.at[row * 2 + 1 - col, rows((1 - core) * 4 + k)]
        pltpu.make_async_copy((first, second)[k // 2].at[k % 2], target, late_sems.at[0, k]).start()
    for distance in (1, 2, 3):
        source_row = (row - distance) & 3
        for k, (ref, index, other_col, other_core, which) in enumerate(pieces):
            slot = source_row * 2 + (1 - col if other_col else col)
            half = 1 - core if other_core else core
            target = layers.at[slot, rows(half * 4 + (which & 3))]
            source = ref.at[index + distance - 1]
            pltpu.make_async_copy(source, target, late_sems.at[distance, k]).start()

    def await_row(source_row):
        distance = (row - source_row) & 3

        def done(k):
            target = layers.at[0, pl.ds(0, PIECE)]
            pltpu.make_async_copy(first.at[0], target, late_sems.at[distance, k]).wait()

        for k in range(4):
            done(k)

        @pl.when(distance > 0)
        def _():
            for k in range(4, len(pieces)):
                done(k)

    def keep(slot):
        return pltpu.make_async_copy(slope.at[slot], slope_out.at[slot], sems.at[slot])

    @pl.when(place[5] == 0)
    def _():
        current[...] = rows_of(arrived)

        def body(slot, carry):
            @pl.when((slot & 1) == 0)
            def _():
                await_row(slot >> 1)

            forward_one(slot, current, layers, slope, left)
            keep(slot).start()
            return carry

        lax.fori_loop(0, STAGE, body, 0)
        for slot in range(STAGE):
            keep(slot).wait()

    @pl.when(place[5] == 1)
    def _():
        for source_row in range(4):
            await_row(source_row)


def middle_kernel(place, hidden, arrived, layers, upstream, factor, current, slope, left, right):
    @pl.when(place[5] == 1)
    def _():
        current[...] = hidden[...]
        upstream[...] = rows_of(arrived)

        def ahead(slot, carry):
            forward_one(slot, current, layers, slope, left)
            return carry

        lax.fori_loop(0, STAGE, ahead, 0)

        def back(step, carry):
            backward_one(STAGE - 1 - step, upstream, layers, slope, right)
            return carry

        lax.fori_loop(0, STAGE, back, 0)
        finish(left, right, factor)


def last_kernel(place, upstream, slope_in, left, late, layers_in, factor, current, slope, right, layers, sems):
    def fetch(slot):
        return (
            pltpu.make_async_copy(slope_in.at[slot], slope.at[slot], sems.at[0, slot]),
            pltpu.make_async_copy(layers_in.at[slot], layers.at[slot], sems.at[1, slot]),
        )

    @pl.when(place[5] == 0)
    def _():
        for slot in reversed(range(STAGE)):
            for copy in fetch(slot):
                copy.start()
        current[...] = upstream[...]

        def back(step, carry):
            slot = STAGE - 1 - step
            for copy in fetch(slot):
                copy.wait()
            backward_one(slot, current, layers, slope, right)
            return carry

        lax.fori_loop(0, STAGE, back, 0)
        finish(left, right, factor)

    @pl.when(place[5] == 1)
    def _():
        factor[...] = late[...]


VMEM = pl.BlockSpec(memory_space=pltpu.VMEM)
SMEM = pl.BlockSpec(memory_space=pltpu.SMEM)
ANY = pl.BlockSpec(memory_space=pl.ANY)
HBM = pl.BlockSpec(memory_space=pltpu.HBM)
PARAMS = pltpu.CompilerParams(vmem_limit_bytes=8 * 1024 * 1024)
SMALL = pltpu.CompilerParams(vmem_limit_bytes=2 * 1024 * 1024)
LARGE = pltpu.CompilerParams(vmem_limit_bytes=30 * 1024 * 1024)
TOKENS = jax.ShapeDtypeStruct((TOK, D), jnp.bfloat16)
SLOPE = jax.ShapeDtypeStruct((STAGE, TOK, D), jnp.float32)
LEFT = jax.ShapeDtypeStruct((STAGE, 2 * RANK, TOK), jnp.float32)
RIGHT = jax.ShapeDtypeStruct((STAGE, TOK, 2 * RANK), jnp.float32)
FACTOR = jax.ShapeDtypeStruct((STAGE, RANK // 2, 2 * RANK), jnp.bfloat16)
LAYERS = jax.ShapeDtypeStruct((STAGE, PACK, D), jnp.bfloat16)
BUNDLE = jax.ShapeDtypeStruct((8, PIECE, D), jnp.bfloat16)


def scratch(shape):
    return pltpu.VMEM(shape.shape, shape.dtype)


def in_hbm(value):
    return pltpu.with_memory_space_constraint(value, pltpu.HBM)


def cost(passes):
    return pl.CostEstimate(
        flops=2 * passes * STAGE * TOK * D * PACK,
        bytes_accessed=STAGE * D * PACK * 2,
        transcendentals=STAGE * TOK * D,
    )


def on_device(inputs, cotangent, weights, proj_in, proj_out, query_factors):
    section, dp = lax.axis_index("section"), lax.axis_index("dp")
    y, col = section // 2, section % 2
    x_hi, z, core = dp // 16, dp // 2 % 8, dp % 2
    stage = y // 4
    quarter = (z + 2 * x_hi) % 4
    way = 1 - 2 * (core ^ x_hi)
    place = jnp.stack([y % 4, col, core, quarter, way, stage]).astype(jnp.int32)

    pack = jnp.concatenate([weights[0], proj_in[0].T, proj_out[0].T])
    rows, beside = gather_rows(pack, core, quarter)

    ahead, seeds = (
        value.reshape(2, 4, TOK, -1).transpose(0, 1, 3, 2).reshape(STAGE, -1, TOK)
        for value in (inputs, cotangent)
    )
    order = [ahead, seeds[4:], seeds[:4]]
    rows[0], order = lax.optimization_barrier((rows[0], jnp.concatenate(order)))
    arrived = lax.all_to_all(order, "section", 0, 0, tiled=True)

    own = jnp.stack(rows)
    own = jnp.stack([own, swap_core(own)])
    queries = query_factors
    queries = jnp.concatenate([queries, swap_core(queries)])
    own, beside, queries = lax.optimization_barrier((own, beside, queries))
    up, side = along_z(own), along_x(own)
    up, side, arrived = lax.optimization_barrier((up, side, arrived))
    turn, two = along_x(up), along_z(up)
    layers, first, second = pl.pallas_call(
        early_kernel,
        out_shape=(LAYERS, BUNDLE, BUNDLE),
        in_specs=[SMEM] + [ANY] * 5,
        out_specs=(VMEM, ANY, ANY),
        scratch_shapes=[pltpu.SemaphoreType.DMA((27,))],
        compiler_params=SMALL,
        cost_estimate=cost(1),
        name="place_early_pieces",
    )(
        place,
        pack,
        in_hbm(beside.reshape(4, PIECE, D)),
        in_hbm(own),
        in_hbm(up.reshape(6, PIECE, D)),
        in_hbm(side.reshape(6, PIECE, D)),
    )
    first, second = swap_core(first), swap_core(second)
    turn, two = lax.optimization_barrier((turn, two))
    turn_other = swap_core(turn)
    hidden, slope, left, layers = pl.pallas_call(
        first_kernel,
        out_shape=(TOKENS, SLOPE, LEFT, LAYERS),
        in_specs=[SMEM, VMEM] + [ANY] * 5 + [VMEM],
        out_specs=(VMEM, HBM, VMEM, VMEM),
        scratch_shapes=[
            scratch(SLOPE),
            pltpu.SemaphoreType.DMA((STAGE,)),
            pltpu.SemaphoreType.DMA((4, 10)),
        ],
        input_output_aliases={7: 3},
        compiler_params=PARAMS,
        cost_estimate=cost(1),
        name="forward_first_stage",
    )(place, arrived, first, second, in_hbm(turn), turn_other, in_hbm(two), layers)
    hidden = move(hidden, lambda x, y, z, c: (x, (y + 2 if y > 1 else y + 6), z, c) if y < 4 else None)
    left, queries = lax.optimization_barrier((left, queries))
    queries = jnp.concatenate([queries, move(queries, lambda x, y, z, c: (x ^ 2, y, z, c))])
    upstream, factor_late = pl.pallas_call(
        middle_kernel,
        out_shape=(TOKENS, FACTOR),
        in_specs=[SMEM, VMEM, VMEM, VMEM],
        out_specs=(VMEM, VMEM),
        scratch_shapes=[scratch(TOKENS), scratch(SLOPE), scratch(LEFT), scratch(RIGHT)],
        compiler_params=PARAMS,
        cost_estimate=cost(2),
        name="second_stage",
    )(place, hidden, arrived, layers)
    upstream = move(upstream, lambda x, y, z, c: (x, (y - 2 if y < 6 else y - 6), z, c) if y > 3 else None)
    upstream, queries = lax.optimization_barrier((upstream, queries))
    factor = pl.pallas_call(
        last_kernel,
        out_shape=FACTOR,
        in_specs=[SMEM, VMEM, HBM, VMEM, VMEM, HBM],
        out_specs=VMEM,
        scratch_shapes=[
            scratch(TOKENS),
            scratch(SLOPE),
            scratch(RIGHT),
            scratch(LAYERS),
            pltpu.SemaphoreType.DMA((2, STAGE)),
        ],
        compiler_params=LARGE,
        cost_estimate=cost(1),
        name="backward_first_stage",
    )(place, upstream, slope, left, factor_late, in_hbm(layers))

    groups = [list(range(8)), list(range(8, 16))]
    parts = lax.all_to_all(factor, "section", 0, 0, tiled=True, axis_index_groups=groups)
    low, high = parts.reshape(2, 4, RANK // 2, 2 * RANK).astype(jnp.float32).sum(1)
    along = [[(h * 8 + k) * 2 + c for k in range(8)] for h in range(2) for c in range(2)]
    sums = jnp.stack([jnp.where(stage == 0, low, high), jnp.where(stage == 0, high, low)])
    sums = sums.astype(jnp.bfloat16)
    sums = lax.all_to_all(
        jnp.broadcast_to(sums[None], (8,) + sums.shape),
        "dp",
        0,
        0,
        tiled=True,
        axis_index_groups=along,
    ).reshape(16, RANK // 2, 2, RANK)
    sums = sums.transpose(0, 2, 1, 3).reshape(16, -1)
    table = lax.dot_general(
        sums, queries.reshape(-1, sums.shape[1]), (((1,), (1,)), ((), ())),
        preferred_element_type=jnp.float32,
    ).reshape(16, 2, 2, -1)
    table = jnp.where(x_hi == 0, table, table[:, ::-1])
    table = jnp.where(core == 0, table, table[:, :, ::-1]).reshape(8, 2, -1)

    table = table.reshape(8, 2, 4, -1).transpose(0, 2, 1, 3)
    outgoing = lax.dynamic_update_slice_in_dim(
        jnp.zeros((16,) + table.shape[1:], jnp.float32), table, x_hi * 8, 0
    ).reshape(64, -1)
    plane = [
        [s * 32 + (h * 8 + k) * 2 + c for s in range(16) for h in range(2) for c in range(2)]
        for k in range(8)
    ]
    scores = lax.all_to_all(outgoing, AXES, 0, 0, tiled=True, axis_index_groups=plane)
    return scores.reshape(32, 4, -1).sum(0).reshape(4, -1)


def solution(mesh):
    placed = (
        P("dp", None, "section"),
        P("dp", None, "section"),
        P("section", None, None),
        P("section", None, None),
        P("section", None, None),
        P("section", "dp", None),
    )
    return jax.shard_map(
        on_device, mesh=mesh, in_specs=placed, out_specs=P("section", "dp"), check_vma=False
    )
```
